256 devices in a mesh: seq: 32 (over y, x, core), head: 8 (over z).
Axes of the slice: x: 4, y: 4, z: 8, core: 2. Of those that a mesh axis runs over, the one named last changes fastest.
Arguments:
- queries: bfloat16 [16384, 4096], P('seq', 'head'), may hold values from -6 to 6
- keys: bfloat16 [16384, 4096], P('seq', 'head'), may hold values from -6 to 6
- values: bfloat16 [16384, 4096], P('seq', 'head'), may hold values from -6 to 6
- gain: float32 [4096], P('head'), may hold values from 0.5 to 2
- out_weight: bfloat16 [4096, 4096], P('seq', 'head'), may hold values from -0.1875 to 0.1875
- cotangent: bfloat16 [16384, 4096], P('seq'), may hold values from -6 to 6
Outputs:
- layer_out: bfloat16 [16384, 4096], P('seq', 'head')
- grad_queries: bfloat16 [16384, 4096], P('seq', 'head')
- grad_keys: bfloat16 [16384, 4096], P('seq', 'head')
- grad_values: bfloat16 [16384, 4096], P('seq', 'head')
- grad_weight: float32 [4096, 4096], P('seq', 'head')
The draws below stay inside these ranges and needn't reach their ends.
All inputs are finite; a program needn't handle non-finite values.
Results may differ from the reference program's by a relative error of at most 0.025.
Values may be sent and summed in bfloat16 or wider, within the bound.
No kernel may reach another device: no remote copies, remote signals or barrier semaphores. Data moves between devices by JAX's collectives and lax.ppermute only.
A program may use at most 128 MiB of HBM per device.

```python
import math
import jax
import jax.numpy as jnp
from jax import lax

D = 4096
H = 32
DH = 128
SPAN = 512
HD = 4096
TOKENS = 16384
N_HEAD = 8


def with_spikes(result, rng, source, target, shards_of, factor):
    def block_of(position):
        return (jnp.arange(result.shape[position]) // (result.shape[position] // shards_of)).reshape((-1,) + (1,) * (result.ndim - 1 - position))

    near = jax.random.permutation(rng, shards_of)[block_of(target)]
    second = (block_of(target) + shards_of // 2) % shards_of
    return jnp.where((block_of(source) == near) | (block_of(source) == second), factor * result, result)


def shard_levels(rng, dims, cuts, least, largest):
    loudness, own = 1.0, jax.random.fold_in(rng, 6)
    for dim, shards_of in cuts:
        heights = jnp.exp(jax.random.uniform(jax.random.fold_in(own, dim), (shards_of,), jnp.float32, least / len(cuts), largest / len(cuts)))
        loudness = loudness * jnp.repeat(heights, dims[dim] // shards_of).reshape([-1 if axis == dim else 1 for axis in range(len(dims))])
    return loudness


def bell_draw(key, dims, scale, reach, cuts=(), held_as=jnp.bfloat16):
    entries = scale * jax.random.normal(key, dims, jnp.float32)
    if cuts:
        entries = entries * shard_levels(key, dims, cuts, -0.22, 0.18)
    return jnp.clip(entries, -reach, reach).astype(held_as)


def heavy_noise(key, shape, width, bound, pieces, heavy, kind=jnp.bfloat16):
    array = width * jax.random.normal(key, shape, jnp.float32)
    if pieces:
        array = array * shard_levels(key, shape, pieces, -0.22, 0.18)
    return jnp.clip(with_spikes(array, jax.random.fold_in(key, 3), *heavy), -bound, bound).astype(kind)


def setup_inputs(seed: int = 0) -> dict:
    seeds = jax.random.split(jax.random.key(seed), 7)
    queries = bell_draw(seeds[0], (TOKENS, HD), 1.0, 6.0, ((0, 32), (1, 8)))
    keys = bell_draw(seeds[1], (TOKENS, HD), 1.0, 6.0, ((0, 32), (1, 8)))
    values = bell_draw(seeds[2], (TOKENS, HD), 1.0, 6.0, ((0, 32), (1, 8)))
    gain = jnp.clip(jnp.exp(math.log(2.0) - 1.3862944 * jax.random.uniform(seeds[3], (HD,), jnp.float32) ** shard_levels(seeds[3], (HD,), ((0, 8),), -0.2, 0.2)), 0.5, 2.0)
    out_weight = heavy_noise(seeds[4], (D, HD), HD ** -0.5, 0.1875, ((0, 32), (1, 8)), (1, 0, 32, 2.75))
    cotangent = heavy_noise(seeds[5], (TOKENS, D), 1.0, 6.0, ((0, 32),), (0, 1, 32, 2.75))
    return dict(queries=queries, keys=keys, values=values, gain=gain, out_weight=out_weight, cotangent=cotangent)


HIGH = lax.Precision.HIGHEST
EPS = 1e-06

def reference(queries, keys, values, gain, out_weight, cotangent):
    tokens = queries.shape[0]
    blocks = tokens // SPAN
    q_blk = queries.reshape(blocks, SPAN, H, DH)
    k_blk = keys.reshape(blocks, SPAN, H, DH)
    v_blk = values.reshape(blocks, SPAN, H, DH)
    causal = jnp.arange(SPAN)[:, None] >= jnp.arange(SPAN)[None, :]

    def block_scores(qb, kb):
        raw = jnp.einsum('thd,shd->hts', qb.astype(jnp.float32), kb.astype(jnp.float32), precision=HIGH)
        return jnp.where(causal[None], raw, 0.0).astype(jnp.bfloat16)

    def forward_step(state, item):
        qb, kb, vb = item
        scores = block_scores(qb, kb)
        intra = jnp.einsum('hts,she->the', scores.astype(jnp.float32), vb.astype(jnp.float32), precision=HIGH)
        inter = jnp.einsum('thd,hde->the', qb.astype(jnp.float32), state, precision=HIGH)
        update = jnp.einsum('thd,the->hde', kb.astype(jnp.float32), vb.astype(jnp.float32), precision=HIGH)
        return (state + update, (intra + inter, state))
    zero_state = jnp.zeros((H, DH, DH), jnp.float32)
    _, (attended, prefixes) = lax.scan(forward_step, zero_state, (q_blk, k_blk, v_blk))
    attended = attended.reshape(tokens, H, DH)
    inv_rms = lax.rsqrt(lax.optimization_barrier(jnp.mean(attended * attended, axis=-1, keepdims=True)) + EPS)
    gain3 = gain.reshape(H, DH)
    normed = (attended * inv_rms * gain3).astype(jnp.bfloat16).reshape(tokens, H * DH)
    group = H * DH // N_HEAD
    total = jnp.zeros((tokens, D), jnp.float32)
    for index in range(N_HEAD):
        cols = slice(index * group, (index + 1) * group)
        partial_out = lax.dot_general(normed[:, cols], out_weight[:, cols], (((1,), (1,)), ((), ())), preferred_element_type=jnp.float32)
        rounded = lax.optimization_barrier(partial_out.astype(jnp.bfloat16))
        total = total + rounded.astype(jnp.float32)
    layer_out = total.astype(jnp.bfloat16)
    grad_normed = jnp.dot(cotangent, out_weight, preferred_element_type=jnp.float32)
    grad_weight = lax.dot_general(cotangent, normed, (((0,), (0,)), ((), ())), preferred_element_type=jnp.float32)
    grad_weight = grad_weight / jnp.sqrt(jnp.float32(tokens))
    scaled = grad_normed.reshape(tokens, H, DH) * gain3
    inner = lax.optimization_barrier(jnp.mean(scaled * attended, axis=-1, keepdims=True))
    grad_att = (inv_rms * (scaled - attended * inv_rms * inv_rms * inner)).astype(jnp.bfloat16)
    g_blk = grad_att.reshape(blocks, SPAN, H, DH)

    def backward_step(state, item):
        qb, kb, vb, gb, prefix = item
        qf = qb.astype(jnp.float32)
        kf = kb.astype(jnp.float32)
        vf = vb.astype(jnp.float32)
        gf = gb.astype(jnp.float32)
        scores = block_scores(qb, kb).astype(jnp.float32)
        raw = jnp.einsum('the,she->hts', gf, vf, precision=HIGH)
        grad_scores = jnp.where(causal[None], raw, 0.0).astype(jnp.bfloat16).astype(jnp.float32)
        dq = jnp.einsum('hts,shd->thd', grad_scores, kf, precision=HIGH) + jnp.einsum('the,hde->thd', gf, prefix, precision=HIGH)
        dk = jnp.einsum('hts,thd->shd', grad_scores, qf, precision=HIGH) + jnp.einsum('she,hde->shd', vf, state, precision=HIGH)
        dv = jnp.einsum('hts,the->she', scores, gf, precision=HIGH) + jnp.einsum('shd,hde->she', kf, state, precision=HIGH)
        update = jnp.einsum('thd,the->hde', qf, gf, precision=HIGH)
        return (state + update, (dq, dk, dv))
    _, (dq, dk, dv) = lax.scan(backward_step, zero_state, (q_blk, k_blk, v_blk, g_blk, prefixes), reverse=True)
    grad_queries = dq.reshape(tokens, H * DH).astype(jnp.bfloat16)
    grad_keys = dk.reshape(tokens, H * DH).astype(jnp.bfloat16)
    grad_values = dv.reshape(tokens, H * DH).astype(jnp.bfloat16)
    return (layer_out, grad_queries, grad_keys, grad_values, grad_weight)
```

```python
import functools

import jax
import jax.numpy as jnp
from jax import lax
from jax.experimental import pallas as pl
from jax.experimental.pallas import tpu as pltpu
from jax.sharding import PartitionSpec as P

DH = 128
SPAN = 512
EPS = 1e-06
NY, NX, NC, NZ = 4, 4, 2, 8
AXES = ("seq", "head")
F32, BF16 = jnp.float32, jnp.bfloat16
NT = (((1,), (1,)), ((), ()))
NN = (((1,), (0,)), ((), ()))
TN = (((0,), (0,)), ((), ()))


def dot(a, b, dims):
    return lax.dot_general(a, b, dims, preferred_element_type=F32)


def pairs(move):
    out = []
    for y in range(NY):
        for x in range(NX):
            for c in range(NC):
                for z in range(NZ):
                    ty, tx, tc, tz = move(y, x, c, z)
                    here = ((y * NX + x) * NC + c) * NZ + z
                    there = (((ty % NY) * NX + tx % NX) * NC + tc) * NZ + tz % NZ
                    out.append((here, there))
    return out


SWAP = pairs(lambda y, x, c, z: (y, x, 1 - c, z))
ALONG_X = {o: pairs(lambda y, x, c, z, o=o: (y, x + o, c, z)) for o in (1, 2, 3)}
ALONG_Y = {o: pairs(lambda y, x, c, z, o=o: (y + o, x, c, z)) for o in (1, 2, 3)}
ALONG_A = {
    o: pairs(lambda y, x, c, z, o=o: (y, x + o, c, z) if c == 0 else (y + o, x, c, z))
    for o in (1, 2, 3)
}
ALONG_B = {
    o: pairs(lambda y, x, c, z, o=o: (y + o, x, c, z) if c == 0 else (y, x + o, c, z))
    for o in (1, 2, 3)
}
RING = pairs(lambda y, x, c, z: (y, x, c, z + 1 if c == 0 else z - 1))


def send(value, perm):
    return lax.ppermute(value, AXES, perm)


def whole(n):
    return [pl.BlockSpec(memory_space=pltpu.VMEM)] * n


def call(kernel, outs, *args, flops=0, vmem=32):
    moved = sum(a.size * a.dtype.itemsize for a in args)
    moved += sum(o.size * o.dtype.itemsize for o in outs)
    return pl.pallas_call(
        kernel,
        out_shape=tuple(outs),
        in_specs=whole(len(args)),
        out_specs=tuple(whole(len(outs))),
        compiler_params=pltpu.CompilerParams(vmem_limit_bytes=vmem * 2**20),
        cost_estimate=pl.CostEstimate(flops=flops, bytes_accessed=moved, transcendentals=0),
    )(*args)


def shape(dims, dtype):
    return jax.ShapeDtypeStruct(dims, dtype)


def head(ref, h, rows=slice(None)):
    return ref[rows, h * DH : (h + 1) * DH]


def states_kernel(a_ref, b_ref, full_ref, sent_ref):
    for h in range(a_ref.shape[1] // DH):
        state = dot(head(a_ref, h), head(b_ref, h), TN)
        full_ref[h] = state
        sent_ref[h] = state.astype(BF16)


def lower(n):
    return lax.broadcasted_iota(jnp.int32, (n, n), 0) >= lax.broadcasted_iota(jnp.int32, (n, n), 1)


HALF = SPAN // 2


def intra_kernel(q_ref, k_ref, v_ref, out_ref):
    keep = lower(HALF)
    lo, hi = slice(0, HALF), slice(HALF, SPAN)
    for h in range(q_ref.shape[1] // DH):
        k0, k1 = head(k_ref, h, lo), head(k_ref, h, hi)
        v0, v1 = head(v_ref, h, lo), head(v_ref, h, hi)
        q0, q1 = head(q_ref, h, lo), head(q_ref, h, hi)
        s00 = jnp.where(keep, dot(q0, k0, NT), 0.0).astype(BF16)
        s10 = dot(q1, k0, NT).astype(BF16)
        s11 = jnp.where(keep, dot(q1, k1, NT), 0.0).astype(BF16)
        out_ref[lo, h * DH : (h + 1) * DH] = dot(s00, v0, NN)
        out_ref[hi, h * DH : (h + 1) * DH] = dot(s10, v0, NN) + dot(s11, v1, NN)


def normed_kernel(intra_ref, q_ref, prefix_ref, gain_ref, att_ref, normed_ref):
    for h in range(q_ref.shape[1] // DH):
        cols = slice(h * DH, (h + 1) * DH)
        att = intra_ref[:, cols] + dot(q_ref[:, cols], prefix_ref[h], NN)
        att_ref[:, cols] = att
        inv = lax.rsqrt(jnp.mean(att * att, axis=-1, keepdims=True) + EPS)
        normed_ref[:, cols] = (att * inv * gain_ref[:, cols]).astype(BF16)


def grad_att_kernel(gn_ref, att_ref, gain_ref, q_ref, g_ref, full_ref, sent_ref):
    for h in range(q_ref.shape[1] // DH):
        cols = slice(h * DH, (h + 1) * DH)
        att = att_ref[:, cols]
        inv = lax.rsqrt(jnp.mean(att * att, axis=-1, keepdims=True) + EPS)
        a = gn_ref[:, cols] * gain_ref[:, cols]
        inner = jnp.mean(a * att, axis=-1, keepdims=True)
        g = (inv * (a - att * (inv * inv * inner))).astype(BF16)
        g_ref[:, cols] = g
        state = dot(q_ref[:, cols], g, TN)
        full_ref[h] = state
        sent_ref[h] = state.astype(BF16)


def back_kernel(q_ref, k_ref, v_ref, g_ref, prefix_ref, dq_ref, dk_ref, dv_ref):
    keep = lower(HALF)
    upper = lax.broadcasted_iota(jnp.int32, (HALF, HALF), 0) <= lax.broadcasted_iota(
        jnp.int32, (HALF, HALF), 1
    )
    lo, hi = slice(0, HALF), slice(HALF, SPAN)
    for h in range(q_ref.shape[1] // DH):
        cols = slice(h * DH, (h + 1) * DH)
        q0, q1 = q_ref[lo, cols], q_ref[hi, cols]
        k0, k1 = k_ref[lo, cols], k_ref[hi, cols]
        v0, v1 = v_ref[lo, cols], v_ref[hi, cols]
        g0, g1 = g_ref[lo, cols], g_ref[hi, cols]
        prefix = prefix_ref[h]
        d00 = jnp.where(keep, dot(g0, v0, NT), 0.0).astype(BF16)
        d10 = dot(g1, v0, NT).astype(BF16)
        d11 = jnp.where(keep, dot(g1, v1, NT), 0.0).astype(BF16)
        dq_ref[lo, cols] = (dot(d00, k0, NN) + dot(g0, prefix, NT)).astype(BF16)
        dq_ref[hi, cols] = (dot(d10, k0, NN) + dot(d11, k1, NN) + dot(g1, prefix, NT)).astype(BF16)
        e00 = jnp.where(upper, dot(v0, g0, NT), 0.0).astype(BF16)
        e01 = dot(v0, g1, NT).astype(BF16)
        e11 = jnp.where(upper, dot(v1, g1, NT), 0.0).astype(BF16)
        dk_ref[lo, cols] = dot(e00, q0, NN) + dot(e01, q1, NN)
        dk_ref[hi, cols] = dot(e11, q1, NN)
        s00 = jnp.where(upper, dot(k0, q0, NT), 0.0).astype(BF16)
        s01 = dot(k0, q1, NT).astype(BF16)
        s11 = jnp.where(upper, dot(k1, q1, NT), 0.0).astype(BF16)
        dv_ref[lo, cols] = dot(s00, g0, NN) + dot(s01, g1, NN)
        dv_ref[hi, cols] = dot(s11, g1, NN)


def finish_kernel(dk_part_ref, dv_part_ref, k_ref, v_ref, suffix_ref, dk_ref, dv_ref):
    for h in range(k_ref.shape[1] // DH):
        cols = slice(h * DH, (h + 1) * DH)
        suffix = suffix_ref[h]
        dk_ref[:, cols] = (dk_part_ref[:, cols] + dot(v_ref[:, cols], suffix, NT)).astype(BF16)
        dv_ref[:, cols] = (dv_part_ref[:, cols] + dot(k_ref[:, cols], suffix, NN)).astype(BF16)


def grad_normed_kernel(cot_ref, w_ref, out_ref):
    part = dot(cot_ref[...], w_ref[...], NN)

    @pl.when(pl.program_id(0) == 0)
    def _():
        out_ref[...] = part

    @pl.when(pl.program_id(0) > 0)
    def _():
        out_ref[...] += part


def grad_normed_of(cotangent, weight):
    tokens, depth = cotangent.shape
    width = weight.shape[1]
    block = 512
    return pl.pallas_call(
        grad_normed_kernel,
        out_shape=shape((tokens, width), F32),
        grid=(depth // block,),
        in_specs=[
            pl.BlockSpec((tokens, block), lambda i: (0, i)),
            pl.BlockSpec((block, width), lambda i: (i, 0)),
        ],
        out_specs=pl.BlockSpec((tokens, width), lambda i: (0, 0)),
        compiler_params=pltpu.CompilerParams(vmem_limit_bytes=32 * 2**20),
        cost_estimate=pl.CostEstimate(
            flops=2 * tokens * depth * width, bytes_accessed=10 * 2**20, transcendentals=0
        ),
    )(cotangent, weight)


def ring_first_kernel(at_ref, normed_ref, w_ref, out_ref):
    out_ref[...] = dot(normed_ref[...], w_ref[...], NT).astype(BF16)


def ring_kernel(at_ref, normed_ref, w_ref, came_ref, out_ref):
    part = dot(normed_ref[...], w_ref[...], NT)
    out_ref[...] = (part + came_ref[...].astype(F32)).astype(BF16)


def ring_step(at, normed, weight, came, part):
    rows, width = normed.shape[0] // 2, normed.shape[1]
    group = weight.shape[0] // NZ
    args = [normed, weight] + ([] if came is None else [came])
    in_specs = [
        pl.BlockSpec((rows, width), lambda i, at: (part, 0)),
        pl.BlockSpec((group, width), lambda i, at: (at[0], 0)),
    ]
    if came is not None:
        in_specs.append(pl.BlockSpec((rows, group), lambda i, at: (0, 0)))
    return pl.pallas_call(
        ring_first_kernel if came is None else ring_kernel,
        out_shape=shape((rows, group), BF16),
        grid_spec=pltpu.PrefetchScalarGridSpec(
            num_scalar_prefetch=1,
            grid=(1,),
            in_specs=in_specs,
            out_specs=pl.BlockSpec((rows, group), lambda i, at: (0, 0)),
        ),
        compiler_params=pltpu.CompilerParams(vmem_limit_bytes=16 * 2**20),
        cost_estimate=pl.CostEstimate(
            flops=2 * rows * group * width, bytes_accessed=2**20, transcendentals=0
        ),
    )(at, *args)


def term_kernel(info_ref, cot_ref, normed_ref, own_ref, other_ref):
    res = dot(cot_ref[...], normed_ref[...], TN).astype(BF16)
    rows = res.shape[0] // 2
    first = info_ref[16] == 0
    own_ref[0] = jnp.where(first, res[:rows], res[rows:])
    other_ref[0] = jnp.where(first, res[rows:], res[:rows])


def terms_of(info, cotangent, normed):
    tokens, depth = cotangent.shape
    width = normed.shape[1]
    chips = NY * NX
    cols = depth // chips
    half = shape((chips, cols // NC, width), BF16)
    return pl.pallas_call(
        term_kernel,
        out_shape=(half, half),
        grid_spec=pltpu.PrefetchScalarGridSpec(
            num_scalar_prefetch=1,
            grid=(4, 4),
            in_specs=[
                pl.BlockSpec((tokens, cols), lambda b, a, info: (0, info[b * 4 + a])),
                pl.BlockSpec((tokens, width), lambda b, a, info: (0, 0)),
            ],
            out_specs=(
                pl.BlockSpec((1, cols // NC, width), lambda b, a, info: (b * 4 + a, 0, 0)),
                pl.BlockSpec((1, cols // NC, width), lambda b, a, info: (a * 4 + b, 0, 0)),
            ),
        ),
        compiler_params=pltpu.CompilerParams(vmem_limit_bytes=32 * 2**20),
        cost_estimate=pl.CostEstimate(
            flops=2 * tokens * depth * width, bytes_accessed=9 * 2**20, transcendentals=0
        ),
    )(info, cotangent, normed)


def place_kernel(rows, at_ref, *refs):
    pieces, out_ref, sems = refs[:-2], refs[-2], refs[-1]
    copies = []
    for p, piece in enumerate(pieces):
        for i in range(4):
            to = pl.multiple_of(at_ref[p * 4 + i] * rows, rows)
            copies.append(
                pltpu.make_async_copy(
                    piece.at[pl.ds(i * rows, rows)], out_ref.at[pl.ds(to, rows)], sems.at[p * 4 + i]
                )
            )
    for copy in copies:
        copy.start()
    for copy in copies:
        copy.wait()


def place(at, pieces):
    rows, width = pieces[0].shape[0] // 4, pieces[0].shape[1]
    n = len(pieces)
    return pl.pallas_call(
        functools.partial(place_kernel, rows),
        out_shape=shape((n * 4 * rows, width), BF16),
        in_specs=[pl.BlockSpec(memory_space=pltpu.SMEM)] + [pl.BlockSpec(memory_space=pl.ANY)] * n,
        out_specs=pl.BlockSpec(memory_space=pl.ANY),
        scratch_shapes=[pltpu.SemaphoreType.DMA((n * 4,))],
        compiler_params=pltpu.CompilerParams(vmem_limit_bytes=16 * 2**20),
        cost_estimate=pl.CostEstimate(flops=0, bytes_accessed=8 * 2**20, transcendentals=0),
    )(at, *pieces)


def line_sums(mine, came, here, reverse):
    total, part = mine, jnp.zeros_like(mine)
    for o in (1, 2, 3):
        value = came[o].astype(F32)
        total = total + value
        source = (here - o) % 4
        part = part + jnp.where(source > here if reverse else source < here, value, 0.0)
    return total, part


def carried(full, sent, y, x, c, reverse):
    half = full.shape[0] // 2
    other = send(sent, SWAP).astype(F32)
    chip = full + other
    mine = jnp.where(c == 0, chip[:half], chip[half:])
    low = mine.astype(BF16)
    row, row_part = line_sums(mine, {o: send(low, ALONG_X[o]) for o in (1, 3, 2)}, x, reverse)
    low = row.astype(BF16)
    _, col_part = line_sums(row, {o: send(low, ALONG_Y[o]) for o in (1, 3, 2)}, y, reverse)
    part = (row_part + col_part).astype(BF16)
    back = send(part, SWAP)
    both = jnp.concatenate([jnp.where(c == 0, part, back), jnp.where(c == 0, back, part)], axis=0)
    extra = jnp.where(c == (0 if reverse else 1), other, 0.0)
    return (both.astype(F32) + extra).astype(BF16)


def gathered(block, y, x, c):
    line = jnp.concatenate([block] + [send(block, ALONG_A[o]) for o in (1, 2, 3)], axis=0)
    own = [line] + [send(line, ALONG_B[o]) for o in (1, 2, 3)]
    other = [send(piece, SWAP) for piece in own]
    at = []
    for core in (c, 1 - c):
        for b in range(4):
            for a in range(4):
                row = jnp.where(core == 0, y - b, y - a) % NY
                col = jnp.where(core == 0, x - a, x - b) % NX
                at.append((row * NX + col) * NC + core)
    return place(jnp.stack(at).astype(jnp.int32), own + other)


def summed_weight(own, other, out_factor):
    _, rows, width = own.shape
    came = send(other, SWAP)
    chip = [
        own[b * 4 : b * 4 + 4].astype(F32) + came[b * 4 : b * 4 + 4].astype(F32) for b in range(4)
    ]
    line = chip[0]
    for o in (1, 3, 2):
        line = line + send(chip[o].astype(BF16), ALONG_B[o]).astype(F32)
    total = line[0]
    for o in (1, 3, 2):
        total = total + send(line[o].astype(BF16), ALONG_A[o]).astype(F32)
    return total * out_factor


def body(queries, keys, values, gain, out_weight, cotangent):
    tokens, width = queries.shape
    heads = width // DH
    s, z = lax.axis_index("seq"), lax.axis_index("head")
    c, x, y = s % NC, (s // NC) % NX, s // (NC * NX)
    state = shape((heads, DH, DH), F32)
    state_low = shape((heads, DH, DH), BF16)
    whole_f32 = shape((tokens, width), F32)
    whole_bf16 = shape((tokens, width), BF16)
    gain2 = gain.reshape(1, width)
    mac = 2 * tokens * width * DH

    full, low = call(states_kernel, (state, state_low), keys, values, flops=mac)
    prefix = carried(full, low, y, x, c, False)
    weight = gathered(out_weight, y, x, c)
    (intra,) = call(intra_kernel, (whole_f32,), queries, keys, values, flops=6 * mac)
    grad_normed = grad_normed_of(cotangent, weight)
    attended, normed = call(
        normed_kernel, (whole_f32, whole_bf16), intra, queries, prefix, gain2, flops=mac
    )

    step = jnp.where(c == 0, 1, -1)
    at = [((z - step * (t + 1)) % NZ).reshape(1).astype(jnp.int32) for t in range(NZ)]
    moving = [ring_step(at[0], normed, weight, None, part) for part in range(2)]

    grad_att, g_full, g_low = call(
        grad_att_kernel,
        (whole_bf16, state, state_low),
        grad_normed, attended, gain2, queries,
        flops=mac,
    )
    suffix = carried(g_full, g_low, y, x, c, True)

    chips = []
    for b in range(4):
        for a in range(4):
            row = jnp.where(c == 0, y + b, y + a) % NY
            col = jnp.where(c == 0, x + a, x + b) % NX
            chips.append(row * NX + col)
    info = jnp.stack(chips + [c]).astype(jnp.int32)
    own, other = terms_of(info, cotangent, normed)
    factor = 1.0 / jnp.sqrt(jnp.float32(tokens * NY * NX * NC))
    grad_weight = summed_weight(own, other, factor)

    grad_queries, dk_part, dv_part = call(
        back_kernel,
        (whole_bf16, whole_f32, whole_f32),
        queries, keys, values, grad_att, prefix,
        flops=20 * mac,
    )
    grad_keys, grad_values = call(
        finish_kernel,
        (whole_bf16, whole_bf16),
        dk_part, dv_part, keys, values, suffix,
        flops=2 * mac,
    )

    for t in range(1, NZ):
        for part in range(2):
            came = send(moving[part], RING)
            moving[part] = ring_step(at[t], normed, weight, came, part)
    layer_out = jnp.concatenate(moving, axis=0)
    return (layer_out, grad_queries, grad_keys, grad_values, grad_weight)


def solution(mesh):
    placed = (
        P("seq", "head"),
        P("seq", "head"),
        P("seq", "head"),
        P("head"),
        P("seq", "head"),
        P("seq", None),
    )
    return jax.shard_map(
        body,
        mesh=mesh,
        in_specs=placed,
        out_specs=(P("seq", "head"),) * 5,
        check_vma=False,
    )
```

```python
import functools

import jax
import jax.numpy as jnp
from jax import lax
from jax.experimental import pallas as pl
from jax.experimental.pallas import tpu as pltpu
from jax.sharding import PartitionSpec as P

DH = 128
SPAN = 512
EPS = 1e-06
ROOM = 16 * 2**20
FREE = pl.CostEstimate(flops=0, bytes_accessed=0, transcendentals=0)
LONGEST = pl.CostEstimate(flops=2 * 10**10, bytes_accessed=0, transcendentals=0)
NY, NX, NC, NZ = 4, 4, 2, 8
AXES = ("seq", "head")
F32, BF16 = jnp.float32, jnp.bfloat16
NT = (((1,), (1,)), ((), ()))
NN = (((1,), (0,)), ((), ()))
TN = (((0,), (0,)), ((), ()))


def dot(a, b, dims):
    return lax.dot_general(a, b, dims, preferred_element_type=F32)


def pairs(move):
    out = []
    for y in range(NY):
        for x in range(NX):
            for c in range(NC):
                for z in range(NZ):
                    ty, tx, tc, tz = move(y, x, c, z)
                    here = ((y * NX + x) * NC + c) * NZ + z
                    there = (((ty % NY) * NX + tx % NX) * NC + tc) * NZ + tz % NZ
                    out.append((here, there))
    return out


SWAP = pairs(lambda y, x, c, z: (y, x, 1 - c, z))
SCAN = (
    pairs(lambda y, x, c, z: (y, x ^ 1, c, z)),
    pairs(lambda y, x, c, z: (y, 3 - x, c, z)),
    pairs(lambda y, x, c, z: (y ^ 1, x, c, z)),
    pairs(lambda y, x, c, z: (3 - y, x, c, z)),
)
ALONG_A = {
    o: pairs(lambda y, x, c, z, o=o: (y, x + o, c, z) if c == 0 else (y + o, x, c, z))
    for o in (1, 2, 3)
}
ALONG_B = {
    o: pairs(lambda y, x, c, z, o=o: (y + o, x, c, z) if c == 0 else (y, x + o, c, z))
    for o in (1, 2, 3)
}
LONG = pairs(lambda y, x, c, z: (y, x, c, z - 1 if c == 0 else z + 1))
SHORT = pairs(lambda y, x, c, z: (y, x, c, z + 1 if c == 0 else z - 1))


def send(value, perm):
    return lax.ppermute(value, AXES, perm)


def after(value, *others):
    return lax.optimization_barrier((value, *others))[0]


def whole(n):
    return [pl.BlockSpec(memory_space=pltpu.VMEM)] * n


def call(kernel, outs, *args, cost=FREE, **extra):
    return pl.pallas_call(
        kernel,
        out_shape=tuple(outs),
        in_specs=whole(len(args)),
        out_specs=tuple(whole(len(outs))),
        compiler_params=pltpu.CompilerParams(vmem_limit_bytes=ROOM),
        cost_estimate=cost,
        **extra,
    )(*args)


def place_of():
    s = lax.axis_index("seq")
    return s >> 3, (s >> 1) & 3, s & 1, lax.axis_index("head")


def shape(dims, dtype):
    return jax.ShapeDtypeStruct(dims, dtype)


def head(ref, h, rows=slice(None)):
    return ref[rows, h * DH : (h + 1) * DH]


def states_kernel(k_ref, v_ref, full_ref, sent_ref):
    for h in range(full_ref.shape[0]):
        state = dot(head(k_ref, h), head(v_ref, h), TN)
        full_ref[h] = state
        sent_ref[h] = state.astype(BF16)


def lower(n):
    return lax.broadcasted_iota(jnp.int32, (n, n), 0) >= lax.broadcasted_iota(jnp.int32, (n, n), 1)


HALF = SPAN // 2


def intra_kernel(q_ref, k_ref, v_ref, out_ref):
    keep = lower(HALF)
    lo, hi = slice(0, HALF), slice(HALF, SPAN)
    for h in range(q_ref.shape[1] // DH):
        k0, k1 = head(k_ref, h, lo), head(k_ref, h, hi)
        v0, v1 = head(v_ref, h, lo), head(v_ref, h, hi)
        q0, q1 = head(q_ref, h, lo), head(q_ref, h, hi)
        s00 = jnp.where(keep, dot(q0, k0, NT), 0.0).astype(BF16)
        s10 = dot(q1, k0, NT).astype(BF16)
        s11 = jnp.where(keep, dot(q1, k1, NT), 0.0).astype(BF16)
        out_ref[lo, h * DH : (h + 1) * DH] = dot(s00, v0, NN)
        out_ref[hi, h * DH : (h + 1) * DH] = dot(s10, v0, NN) + dot(s11, v1, NN)


def normed_kernel(intra_ref, q_ref, prefix_ref, gain_ref, att_ref, normed_ref, turned_ref):
    for h in range(q_ref.shape[1] // DH):
        cols = slice(h * DH, (h + 1) * DH)
        att = intra_ref[:, cols] + dot(q_ref[:, cols], prefix_ref[h], NN)
        att_ref[:, cols] = att
        inv = lax.rsqrt(jnp.mean(att * att, axis=-1, keepdims=True) + EPS)
        normed = (att * inv * gain_ref[:, cols]).astype(BF16)
        normed_ref[:, cols] = normed
        turned_ref[cols, :] = normed.T


def grad_att_kernel(gn_ref, att_ref, gain_ref, q_ref, g_ref, full_ref, sent_ref):
    for h in range(q_ref.shape[1] // DH):
        cols = slice(h * DH, (h + 1) * DH)
        att = att_ref[:, cols]
        inv = lax.rsqrt(jnp.mean(att * att, axis=-1, keepdims=True) + EPS)
        a = gn_ref[:, cols] * gain_ref[:, cols]
        inner = jnp.mean(a * att, axis=-1, keepdims=True)
        g = (inv * (a - att * (inv * inv * inner))).astype(BF16)
        g_ref[:, cols] = g
        state = dot(q_ref[:, cols], g, TN)
        full_ref[h] = state
        sent_ref[h] = state.astype(BF16)


def back_kernel(q_ref, k_ref, v_ref, g_ref, prefix_ref, dq_ref, dk_ref, dv_ref):
    keep = lower(HALF)
    upper = lax.broadcasted_iota(jnp.int32, (HALF, HALF), 0) <= lax.broadcasted_iota(
        jnp.int32, (HALF, HALF), 1
    )
    lo, hi = slice(0, HALF), slice(HALF, SPAN)
    for h in range(q_ref.shape[1] // DH):
        cols = slice(h * DH, (h + 1) * DH)
        q0, q1 = q_ref[lo, cols], q_ref[hi, cols]
        k0, k1 = k_ref[lo, cols], k_ref[hi, cols]
        v0, v1 = v_ref[lo, cols], v_ref[hi, cols]
        g0, g1 = g_ref[lo, cols], g_ref[hi, cols]
        prefix = prefix_ref[h]
        d00 = jnp.where(keep, dot(g0, v0, NT), 0.0).astype(BF16)
        d10 = dot(g1, v0, NT).astype(BF16)
        d11 = jnp.where(keep, dot(g1, v1, NT), 0.0).astype(BF16)
        dq_ref[lo, cols] = (dot(d00, k0, NN) + dot(g0, prefix, NT)).astype(BF16)
        dq_ref[hi, cols] = (dot(d10, k0, NN) + dot(d11, k1, NN) + dot(g1, prefix, NT)).astype(BF16)
        e00 = jnp.where(upper, dot(v0, g0, NT), 0.0).astype(BF16)
        e01 = dot(v0, g1, NT).astype(BF16)
        e11 = jnp.where(upper, dot(v1, g1, NT), 0.0).astype(BF16)
        dk_ref[lo, cols] = dot(e00, q0, NN) + dot(e01, q1, NN)
        dk_ref[hi, cols] = dot(e11, q1, NN)
        s00 = jnp.where(upper, dot(k0, q0, NT), 0.0).astype(BF16)
        s01 = dot(k0, q1, NT).astype(BF16)
        s11 = jnp.where(upper, dot(k1, q1, NT), 0.0).astype(BF16)
        dv_ref[lo, cols] = dot(s00, g0, NN) + dot(s01, g1, NN)
        dv_ref[hi, cols] = dot(s11, g1, NN)


def finish_kernel(dk_part_ref, dv_part_ref, k_ref, v_ref, suffix_ref, dk_ref, dv_ref):
    for h in range(k_ref.shape[1] // DH):
        cols = slice(h * DH, (h + 1) * DH)
        suffix = suffix_ref[h]
        dk_ref[:, cols] = (dk_part_ref[:, cols] + dot(v_ref[:, cols], suffix, NT)).astype(BF16)
        dv_ref[:, cols] = (dv_part_ref[:, cols] + dot(k_ref[:, cols], suffix, NN)).astype(BF16)


def grad_normed_kernel(cot_ref, w_ref, out_ref):
    block = 1024

    def lap(i, _):
        at = pl.multiple_of(i * block, block)
        part = dot(cot_ref[:, pl.ds(at, block)], w_ref[pl.ds(at, block), :], NN)

        @pl.when(i == 0)
        def _():
            out_ref[...] = part

        @pl.when(i > 0)
        def _():
            out_ref[...] += part

        return 0

    lax.fori_loop(0, cot_ref.shape[1] // block, lap, 0)


def ring_kernel(away, normed_ref, w_ref, *refs):
    group = normed_ref.shape[1]
    _, _, core, z = place_of()
    owner = (z + jnp.where(core == 0, -away, away)) & (NZ - 1)
    rows = pl.ds(pl.multiple_of(owner * group, group), group)
    part = dot(normed_ref[...], w_ref[rows, :], NT)
    for came_ref in refs[:-1]:
        part = part + came_ref[...].astype(F32)
    refs[-1][...] = part.astype(BF16)


def ring_step(away, normed, weight, *came):
    out = shape(normed.shape, BF16)
    kernel = functools.partial(ring_kernel, away)
    return call(kernel, (out,), normed, weight, *came, cost=LONGEST)[0]


def chip_at(b, a, at):
    y, x, core, _ = at
    row = (y + jnp.where(core == 0, b, a)) & 3
    col = (x + jnp.where(core == 0, a, b)) & 3
    return row * NX + col


def terms_kernel(turned_ref, cot_ref, own_ref, other_ref):
    at = place_of()
    first = at[2] == 0
    cols = own_ref.shape[2]

    def lap(b, _):
        for a in range(4):
            start = pl.multiple_of(chip_at(b, a, at) * (NC * cols), NC * cols)
            res = dot(turned_ref[...], cot_ref[:, pl.ds(start, NC * cols)], NN).astype(BF16)
            lo, hi = res[:, :cols], res[:, cols:]
            own_ref[b * 4 + a] = jnp.where(first, lo, hi)
            other_ref[b * 4 + a] = jnp.where(first, hi, lo)
        return 0

    lax.fori_loop(0, 4, lap, 0)


def terms_of(cotangent, turned):
    chips = NY * NX
    half = shape((chips, turned.shape[0], cotangent.shape[1] // chips // NC), BF16)
    return call(terms_kernel, (half, half), turned, cotangent)


def chip_sum_kernel(own_ref, came_ref, here_ref, up_ref, far_lo_ref, far_hi_ref, down_ref):
    for b in range(4):
        for a in range(4):
            total = own_ref[b * 4 + a].astype(F32) + came_ref[a * 4 + b].astype(F32)
            total = total.astype(BF16)
            if b == 2:
                (far_lo_ref if a < 2 else far_hi_ref)[a % 2] = total
            else:
                (here_ref, up_ref, None, down_ref)[b][a] = total


def relay_kernel(up_ref, down_ref, lo_ref, hi_ref, up_out_ref, down_out_ref):
    for a in range(4):
        if a < 2:
            up_out_ref[a] = (up_ref[a].astype(F32) + lo_ref[a].astype(F32)).astype(BF16)
            down_out_ref[a] = down_ref[a]
        else:
            up_out_ref[a] = up_ref[a]
            down_out_ref[a] = (down_ref[a].astype(F32) + hi_ref[a - 2].astype(F32)).astype(BF16)


def line_sum_kernel(own_ref, *refs):
    came, outs = refs[:2], refs[2:]
    for a in range(4):
        total = own_ref[a].astype(F32)
        for ref in came:
            total = total + ref[a].astype(F32)
        outs[a][...] = total.astype(BF16)


def last_sum_kernel(factor, own_ref, a_ref, b_ref, c_ref, out_ref):
    total = own_ref[...].astype(F32)
    for ref in (a_ref, b_ref, c_ref):
        total = total + ref[...].astype(F32)
    out_ref[...] = total.T * factor


def line_slots(_):
    y, x, core, _ = place_of()
    here = jnp.where(core == 0, x, y)
    return [(here - o) & 3 for o in range(4)]


def gather_slots(other, b):
    y, x, core, _ = place_of()
    core = 1 - core if other else core
    out = []
    for a in range(4):
        row = jnp.where(core == 0, (y + b) & 3, a)
        col = jnp.where(core == 0, a, (x + b) & 3)
        out.append((row * NX + col) * NC + core)
    return out


def place_kernel(rows, counts, slots, lines, *refs):
    out_ref = refs[-1]
    places = [p for line in lines for p in slots(line)]
    n = 0
    for piece, count in zip(refs, counts):
        for i in range(count):
            to = pl.multiple_of(places[n] * rows, rows)
            out_ref[pl.ds(to, rows), :] = piece[i * rows : (i + 1) * rows, :]
            n += 1


def place(rows, total, slots, lines, pieces, into=None, cost=FREE):
    counts = tuple(p.shape[0] // rows for p in pieces)
    kernel = functools.partial(place_kernel, rows, counts, slots, lines)
    out = shape((total, pieces[0].shape[1]), BF16)
    if into is None:
        return call(kernel, (out,), *pieces, cost=cost)[0]
    return call(kernel, (out,), *pieces, into, input_output_aliases={len(pieces): 0})[0]


def scan_begin_kernel(full_ref, came_ref, total_ref, low_ref):
    half = total_ref.shape[0]
    first = place_of()[2] * half
    for h in range(half):
        total = full_ref[first + h] + came_ref[first + h].astype(F32)
        total_ref[h] = total
        low_ref[h] = total.astype(BF16)


def scan_kernel(step, reverse, total_ref, part_ref, came_ref, total_out, part_out, low_ref):
    line = place_of()[0 if step >= 2 else 1]
    behind = (line & 1) if step % 2 == 0 else line >> 1
    counts = (1 - behind if reverse else behind).astype(F32)
    for h in range(total_ref.shape[0]):
        came = came_ref[h].astype(F32)
        total = total_ref[h] + came
        total_out[h] = total
        part_out[h] = came * counts if step == 0 else part_ref[h] + came * counts
        low_ref[h] = (part_out[h] if step == 3 else total).astype(BF16)


def scan_end_kernel(reverse, part_ref, back_ref, other_ref, out_ref):
    half = part_ref.shape[0]
    core = place_of()[2]
    own = core * half
    counts = (1 - core if reverse else core).astype(F32)
    for h in range(half):
        other = other_ref[own + h].astype(F32) * counts
        out_ref[own + h] = (part_ref[h] + other).astype(BF16)
        other = other_ref[half - own + h].astype(F32) * counts
        out_ref[half - own + h] = (back_ref[h].astype(F32) + other).astype(BF16)


class Scan:

    def __init__(self, reverse):
        self.reverse = reverse

    def begin(self, full, low, *others):
        self.other = send(low, SWAP)
        half = (full.shape[0] // 2, *full.shape[1:])
        self.f32, self.bf16 = shape(half, F32), shape(half, BF16)
        self.total, self.low = call(
            scan_begin_kernel, (self.f32, self.bf16), after(full, *others), self.other
        )
        self.part = self.total

    def step(self, i, first=(), then=()):
        came = send(after(self.low, *first), SCAN[i])
        self.total, self.part, self.low = call(
            functools.partial(scan_kernel, i, self.reverse),
            (self.f32, self.f32, self.bf16),
            after(self.total, *then), self.part, came,
        )

    def end(self, *others):
        back = send(after(self.low, *others), SWAP)
        return call(
            functools.partial(scan_end_kernel, self.reverse),
            (shape(self.other.shape, BF16),),
            self.part, back, self.other,
        )[0]


def halves_kernel(a_ref, b_ref, lo_ref, hi_ref):
    rows = lo_ref.shape[0]
    lo_ref[...] = a_ref[:rows]
    hi_ref[...] = b_ref[rows:]


def chip_sums(own, came):
    _, width, cols = own.shape
    full, half = shape((4, width, cols), BF16), shape((2, width, cols), BF16)
    return call(chip_sum_kernel, (full, full, half, half, full), own, came)


def line_sums(own, *lines):
    _, width, cols = own.shape
    return call(line_sum_kernel, (shape((width, cols), BF16),) * 4, own, *lines)


def last_sum(lines, factor):
    width, cols = lines[0].shape
    kernel = functools.partial(last_sum_kernel, factor)
    return call(kernel, (shape((cols, width), F32),), *lines)[0]


def body(queries, keys, values, gain, out_weight, cotangent):
    tokens, width = queries.shape
    heads = width // DH
    state = shape((heads, DH, DH), F32)
    state_low = shape((heads, DH, DH), BF16)
    whole_f32 = shape((tokens, width), F32)
    whole_bf16 = shape((tokens, width), BF16)
    gain2 = gain.reshape(1, width)

    rows = out_weight.shape[0]
    came = [send(out_weight, ALONG_A[o]) for o in (1, 2, 3)]
    full, low = call(states_kernel, (state, state_low), keys, values)
    line = place(rows, 4 * rows, line_slots, (0,), [after(out_weight, low), *came], cost=LONGEST)
    scan = Scan(False)
    scan.begin(full, low, line)
    scan.step(0)
    scan.step(1)
    before, behind = send(line, ALONG_B[1]), send(line, ALONG_B[3])
    scan.step(2)
    (intra,) = call(intra_kernel, (whole_f32,), queries, keys, values)
    half_line = shape((2 * rows, width), BF16)
    lo, hi = call(halves_kernel, (half_line, half_line), before, behind)
    scan.step(3, (lo, intra))
    far_lo, far_hi = send(lo, ALONG_B[1]), send(hi, ALONG_B[3])
    own = [line, before, behind, far_lo, far_hi]
    other = [send(piece, SWAP) for piece in own]
    prefix = scan.end(far_lo, far_hi)
    size = rows * NY * NX * NC
    weight = place(rows, size, functools.partial(gather_slots, False), (0, 3, 1, 2), own)
    weight = place(
        rows, size, functools.partial(gather_slots, True), (0, 3, 1, 2), other, into=weight
    )
    attended, normed, turned = call(
        normed_kernel,
        (whole_f32, whole_bf16, shape((width, tokens), BF16)),
        intra, queries, prefix, gain2,
    )

    long = ring_step(4, normed, weight)
    short = ring_step(-3, normed, weight)
    own, other = terms_of(cotangent, after(turned, long, short))
    grad_normed = call(grad_normed_kernel, (whole_f32,), after(cotangent, own), weight)[0]
    grad_att, g_full, g_low = call(
        grad_att_kernel, (whole_bf16, state, state_low), grad_normed, attended, gain2, queries
    )

    came = lax.optimization_barrier((send(long, LONG), send(short, SHORT)))
    ready = after(normed, grad_att)
    long = ring_step(3, ready, weight, came[0])
    short = ring_step(-2, ready, weight, came[1])
    scan = Scan(True)
    scan.begin(g_full, g_low, long, short)
    scan.step(0)
    grad_queries, dk_part, dv_part = call(
        back_kernel,
        (whole_bf16, whole_f32, whole_f32),
        queries, keys, values, after(grad_att, long, short), prefix,
    )
    here, up, far_lo, far_hi, down = chip_sums(after(own, scan.total), send(other, SWAP))
    far = send(far_lo, ALONG_B[1]), send(far_hi, ALONG_B[3])

    came = lax.optimization_barrier((send(long, LONG), send(short, SHORT)))
    ready = after(normed, here, dk_part)
    long = ring_step(2, ready, weight, came[0])
    short = ring_step(-1, ready, weight, came[1])
    scan.step(1, then=(long, short))
    scan.step(2)
    up = after(up, long, short)
    up, down = call(relay_kernel, (shape(up.shape, BF16),) * 2, up, down, *far)
    near = send(up, ALONG_B[1]), send(down, ALONG_B[3])
    line = line_sums(after(here, long, short), *near)

    came = lax.optimization_barrier((send(long, LONG), send(short, SHORT)))
    ready = after(normed, scan.total, line[0])
    long = ring_step(1, ready, weight, came[0])
    scan.step(3, then=(long,))
    last = [send(line[o], ALONG_A[o]) for o in (1, 3, 2)]
    suffix = scan.end()
    grad_keys, grad_values = call(
        finish_kernel, (whole_bf16, whole_bf16), dk_part, dv_part, keys, values, suffix
    )
    grad_weight = last_sum([after(line[0], long), *last], (tokens * NY * NX * NC) ** -0.5)
    layer_out = ring_step(0, normed, weight, send(long, LONG), came[1])
    return (layer_out, grad_queries, grad_keys, grad_values, grad_weight)


def solution(mesh):
    placed = (
        P("seq", "head"),
        P("seq", "head"),
        P("seq", "head"),
        P("head"),
        P("seq", "head"),
        P("seq", None),
    )
    return jax.shard_map(
        body,
        mesh=mesh,
        in_specs=placed,
        out_specs=(P("seq", "head"),) * 5,
        check_vma=False,
    )
```

```python
import functools

import jax
import jax.numpy as jnp
from jax import lax
from jax.experimental import pallas as pl
from jax.experimental.pallas import tpu as pltpu
from jax.sharding import PartitionSpec as P

DH = 128
SPAN = 512
EPS = 1e-06
ROOM = 16 * 2**20
FREE = pl.CostEstimate(flops=0, bytes_accessed=0, transcendentals=0)
LONGEST = pl.CostEstimate(flops=2 * 10**10, bytes_accessed=0, transcendentals=0)
NY, NX, NC, NZ = 4, 4, 2, 8
AXES = ("seq", "head")
F32, BF16 = jnp.float32, jnp.bfloat16
NT = (((1,), (1,)), ((), ()))
NN = (((1,), (0,)), ((), ()))
TN = (((0,), (0,)), ((), ()))


def dot(a, b, dims):
    return lax.dot_general(a, b, dims, preferred_element_type=F32)


def pairs(move):
    out = []
    for y in range(NY):
        for x in range(NX):
            for c in range(NC):
                for z in range(NZ):
                    ty, tx, tc, tz = move(y, x, c, z)
                    here = ((y * NX + x) * NC + c) * NZ + z
                    there = (((ty % NY) * NX + tx % NX) * NC + tc) * NZ + tz % NZ
                    out.append((here, there))
    return out


SWAP = pairs(lambda y, x, c, z: (y, x, 1 - c, z))
SCAN = (
    pairs(lambda y, x, c, z: (y, x ^ 1, c, z)),
    pairs(lambda y, x, c, z: (y, 3 - x, c, z)),
    pairs(lambda y, x, c, z: (y ^ 1, x, c, z)),
    pairs(lambda y, x, c, z: (3 - y, x, c, z)),
)
ALONG_A = {
    o: pairs(lambda y, x, c, z, o=o: (y, x + o, c, z) if c == 0 else (y + o, x, c, z))
    for o in (1, 2, 3)
}
ALONG_B = {
    o: pairs(lambda y, x, c, z, o=o: (y + o, x, c, z) if c == 0 else (y, x + o, c, z))
    for o in (1, 2, 3)
}
LONG = pairs(lambda y, x, c, z: (y, x, c, z - 1 if c == 0 else z + 1))
SHORT = pairs(lambda y, x, c, z: (y, x, c, z + 1 if c == 0 else z - 1))


def send(value, perm):
    return lax.ppermute(value, AXES, perm)


def after(value, *others):
    return lax.optimization_barrier((value, *others))[0]


def whole(n):
    return [pl.BlockSpec(memory_space=pltpu.VMEM)] * n


def call(kernel, outs, *args, cost=FREE, **extra):
    return pl.pallas_call(
        kernel,
        out_shape=tuple(outs),
        in_specs=whole(len(args)),
        out_specs=tuple(whole(len(outs))),
        compiler_params=pltpu.CompilerParams(vmem_limit_bytes=ROOM),
        cost_estimate=cost,
        **extra,
    )(*args)


def place_of():
    s = lax.axis_index("seq")
    return s >> 3, (s >> 1) & 3, s & 1, lax.axis_index("head")


def shape(dims, dtype):
    return jax.ShapeDtypeStruct(dims, dtype)


def head(ref, h, rows=slice(None)):
    return ref[rows, h * DH : (h + 1) * DH]


def states_kernel(k_ref, v_ref, full_ref, sent_ref):
    for h in range(full_ref.shape[0]):
        state = dot(head(k_ref, h), head(v_ref, h), TN)
        full_ref[h] = state
        sent_ref[h] = state.astype(BF16)


def lower(n):
    return lax.broadcasted_iota(jnp.int32, (n, n), 0) >= lax.broadcasted_iota(jnp.int32, (n, n), 1)


HALF = SPAN // 2


def intra_kernel(q_ref, k_ref, v_ref, out_ref):
    keep = lower(HALF)
    lo, hi = slice(0, HALF), slice(HALF, SPAN)
    for h in range(q_ref.shape[1] // DH):
        k0, k1 = head(k_ref, h, lo), head(k_ref, h, hi)
        v0, v1 = head(v_ref, h, lo), head(v_ref, h, hi)
        q0, q1 = head(q_ref, h, lo), head(q_ref, h, hi)
        s00 = jnp.where(keep, dot(q0, k0, NT), 0.0).astype(BF16)
        s10 = dot(q1, k0, NT).astype(BF16)
        s11 = jnp.where(keep, dot(q1, k1, NT), 0.0).astype(BF16)
        out_ref[lo, h * DH : (h + 1) * DH] = dot(s00, v0, NN)
        out_ref[hi, h * DH : (h + 1) * DH] = dot(s10, v0, NN) + dot(s11, v1, NN)


def normed_kernel(intra_ref, q_ref, prefix_ref, gain_ref, att_ref, normed_ref, turned_ref):
    for h in range(q_ref.shape[1] // DH):
        cols = slice(h * DH, (h + 1) * DH)
        att = intra_ref[:, cols] + dot(q_ref[:, cols], prefix_ref[h], NN)
        att_ref[:, cols] = att
        inv = lax.rsqrt(jnp.mean(att * att, axis=-1, keepdims=True) + EPS)
        normed = (att * inv * gain_ref[:, cols]).astype(BF16)
        normed_ref[:, cols] = normed
        turned_ref[cols, :] = normed.T


def grad_att_kernel(gn_ref, att_ref, gain_ref, q_ref, g_ref, full_ref, sent_ref):
    for h in range(q_ref.shape[1] // DH):
        cols = slice(h * DH, (h + 1) * DH)
        att = att_ref[:, cols]
        inv = lax.rsqrt(jnp.mean(att * att, axis=-1, keepdims=True) + EPS)
        a = gn_ref[:, cols] * gain_ref[:, cols]
        inner = jnp.mean(a * att, axis=-1, keepdims=True)
        g = (inv * (a - att * (inv * inv * inner))).astype(BF16)
        g_ref[:, cols] = g
        state = dot(q_ref[:, cols], g, TN)
        full_ref[h] = state
        sent_ref[h] = state.astype(BF16)


def back_kernel(q_ref, k_ref, v_ref, g_ref, prefix_ref, dq_ref, dk_ref, dv_ref):
    keep = lower(HALF)
    upper = lax.broadcasted_iota(jnp.int32, (HALF, HALF), 0) <= lax.broadcasted_iota(
        jnp.int32, (HALF, HALF), 1
    )
    lo, hi = slice(0, HALF), slice(HALF, SPAN)
    for h in range(q_ref.shape[1] // DH):
        cols = slice(h * DH, (h + 1) * DH)
        q0, q1 = q_ref[lo, cols], q_ref[hi, cols]
        k0, k1 = k_ref[lo, cols], k_ref[hi, cols]
        v0, v1 = v_ref[lo, cols], v_ref[hi, cols]
        g0, g1 = g_ref[lo, cols], g_ref[hi, cols]
        prefix = prefix_ref[h]
        d00 = jnp.where(keep, dot(g0, v0, NT), 0.0).astype(BF16)
        d10 = dot(g1, v0, NT).astype(BF16)
        d11 = jnp.where(keep, dot(g1, v1, NT), 0.0).astype(BF16)
        dq_ref[lo, cols] = (dot(d00, k0, NN) + dot(g0, prefix, NT)).astype(BF16)
        dq_ref[hi, cols] = (dot(d10, k0, NN) + dot(d11, k1, NN) + dot(g1, prefix, NT)).astype(BF16)
        e00 = jnp.where(upper, dot(v0, g0, NT), 0.0).astype(BF16)
        e01 = dot(v0, g1, NT).astype(BF16)
        e11 = jnp.where(upper, dot(v1, g1, NT), 0.0).astype(BF16)
        dk_ref[lo, cols] = dot(e00, q0, NN) + dot(e01, q1, NN)
        dk_ref[hi, cols] = dot(e11, q1, NN)
        s00 = jnp.where(upper, dot(k0, q0, NT), 0.0).astype(BF16)
        s01 = dot(k0, q1, NT).astype(BF16)
        s11 = jnp.where(upper, dot(k1, q1, NT), 0.0).astype(BF16)
        dv_ref[lo, cols] = dot(s00, g0, NN) + dot(s01, g1, NN)
        dv_ref[hi, cols] = dot(s11, g1, NN)


def finish_kernel(dk_part_ref, dv_part_ref, k_ref, v_ref, suffix_ref, dk_ref, dv_ref):
    for h in range(k_ref.shape[1] // DH):
        cols = slice(h * DH, (h + 1) * DH)
        suffix = suffix_ref[h]
        dk_ref[:, cols] = (dk_part_ref[:, cols] + dot(v_ref[:, cols], suffix, NT)).astype(BF16)
        dv_ref[:, cols] = (dv_part_ref[:, cols] + dot(k_ref[:, cols], suffix, NN)).astype(BF16)


def grad_normed_kernel(cot_ref, w_ref, out_ref):
    block = 1024

    def lap(i, _):
        at = pl.multiple_of(i * block, block)
        part = dot(cot_ref[:, pl.ds(at, block)], w_ref[pl.ds(at, block), :], NN)

        @pl.when(i == 0)
        def _():
            out_ref[...] = part

        @pl.when(i > 0)
        def _():
            out_ref[...] += part

        return 0

    lax.fori_loop(0, cot_ref.shape[1] // block, lap, 0)


def ring_kernel(away, normed_ref, w_ref, *refs):
    group = normed_ref.shape[1]
    _, _, core, z = place_of()
    owner = (z + jnp.where(core == 0, -away, away)) & (NZ - 1)
    rows = pl.ds(pl.multiple_of(owner * group, group), group)
    part = dot(normed_ref[...], w_ref[rows, :], NT)
    for came_ref in refs[:-1]:
        part = part + came_ref[...].astype(F32)
    refs[-1][...] = part.astype(BF16)


def ring_step(away, normed, weight, *came, cost=FREE):
    out = shape(normed.shape, BF16)
    kernel = functools.partial(ring_kernel, away)
    return call(kernel, (out,), normed, weight, *came, cost=cost)[0]


def chip_at(b, a, at):
    y, x, core, _ = at
    row = (y + jnp.where(core == 0, b, a)) & 3
    col = (x + jnp.where(core == 0, a, b)) & 3
    return row * NX + col


def terms_kernel(turned_ref, cot_ref, own_ref, other_ref):
    at = place_of()
    first = at[2] == 0
    cols = own_ref.shape[2]

    def lap(b, _):
        for a in range(4):
            start = pl.multiple_of(chip_at(b, a, at) * (NC * cols), NC * cols)
            res = dot(turned_ref[...], cot_ref[:, pl.ds(start, NC * cols)], NN).astype(BF16)
            lo, hi = res[:, :cols], res[:, cols:]
            own_ref[b * 4 + a] = jnp.where(first, lo, hi)
            other_ref[b * 4 + a] = jnp.where(first, hi, lo)
        return 0

    lax.fori_loop(0, 4, lap, 0)


def terms_of(cotangent, turned):
    chips = NY * NX
    half = shape((chips, turned.shape[0], cotangent.shape[1] // chips // NC), BF16)
    return call(terms_kernel, (half, half), turned, cotangent)


def chip_sum_kernel(own_ref, came_ref, here_ref, up_ref, far_lo_ref, far_hi_ref, down_ref):
    for b in range(4):
        for a in range(4):
            total = own_ref[b * 4 + a].astype(F32) + came_ref[a * 4 + b].astype(F32)
            total = total.astype(BF16)
            if b == 2:
                (far_lo_ref if a < 2 else far_hi_ref)[a % 2] = total
            else:
                (here_ref, up_ref, None, down_ref)[b][a] = total


def relay_kernel(up_ref, down_ref, lo_ref, hi_ref, up_out_ref, down_out_ref):
    for a in range(4):
        if a < 2:
            up_out_ref[a] = (up_ref[a].astype(F32) + lo_ref[a].astype(F32)).astype(BF16)
            down_out_ref[a] = down_ref[a]
        else:
            up_out_ref[a] = up_ref[a]
            down_out_ref[a] = (down_ref[a].astype(F32) + hi_ref[a - 2].astype(F32)).astype(BF16)


def line_sum_kernel(own_ref, *refs):
    came, outs = refs[:2], refs[2:]
    for a in range(4):
        total = own_ref[a].astype(F32)
        for ref in came:
            total = total + ref[a].astype(F32)
        outs[a][...] = total.astype(BF16)


def last_sum_kernel(factor, own_ref, a_ref, b_ref, c_ref, out_ref):
    total = own_ref[...].astype(F32)
    for ref in (a_ref, b_ref, c_ref):
        total = total + ref[...].astype(F32)
    out_ref[...] = total.T * factor


def line_slots(_):
    y, x, core, _ = place_of()
    here = jnp.where(core == 0, x, y)
    return [(here - o) & 3 for o in range(4)]


def gather_slots(other, b):
    y, x, core, _ = place_of()
    core = 1 - core if other else core
    out = []
    for a in range(4):
        row = jnp.where(core == 0, (y + b) & 3, a)
        col = jnp.where(core == 0, a, (x + b) & 3)
        out.append((row * NX + col) * NC + core)
    return out


def place_kernel(rows, counts, slots, lines, *refs):
    out_ref = refs[-1]
    places = [p for line in lines for p in slots(line)]
    n = 0
    for piece, count in zip(refs, counts):
        for i in range(count):
            to = pl.multiple_of(places[n] * rows, rows)
            out_ref[pl.ds(to, rows), :] = piece[i * rows : (i + 1) * rows, :]
            n += 1


def place(rows, total, slots, lines, pieces, into=None, cost=FREE):
    counts = tuple(p.shape[0] // rows for p in pieces)
    kernel = functools.partial(place_kernel, rows, counts, slots, lines)
    out = shape((total, pieces[0].shape[1]), BF16)
    if into is None:
        return call(kernel, (out,), *pieces, cost=cost)[0]
    return call(kernel, (out,), *pieces, into, input_output_aliases={len(pieces): 0})[0]


def scan_begin_kernel(full_ref, came_ref, total_ref, low_ref):
    half = total_ref.shape[0]
    first = place_of()[2] * half
    for h in range(half):
        total = full_ref[first + h] + came_ref[first + h].astype(F32)
        total_ref[h] = total
        low_ref[h] = total.astype(BF16)


def scan_kernel(step, reverse, total_ref, part_ref, came_ref, total_out, part_out, low_ref):
    line = place_of()[0 if step >= 2 else 1]
    behind = (line & 1) if step % 2 == 0 else line >> 1
    counts = (1 - behind if reverse else behind).astype(F32)
    for h in range(total_ref.shape[0]):
        came = came_ref[h].astype(F32)
        total = total_ref[h] + came
        total_out[h] = total
        part_out[h] = came * counts if step == 0 else part_ref[h] + came * counts
        low_ref[h] = (part_out[h] if step == 3 else total).astype(BF16)


def scan_end_kernel(reverse, part_ref, back_ref, other_ref, out_ref):
    half = part_ref.shape[0]
    core = place_of()[2]
    own = core * half
    counts = (1 - core if reverse else core).astype(F32)
    for h in range(half):
        other = other_ref[own + h].astype(F32) * counts
        out_ref[own + h] = (part_ref[h] + other).astype(BF16)
        other = other_ref[half - own + h].astype(F32) * counts
        out_ref[half - own + h] = (back_ref[h].astype(F32) + other).astype(BF16)


class Scan:

    def __init__(self, reverse):
        self.reverse = reverse

    def begin(self, full, low, *others):
        self.other = send(low, SWAP)
        half = (full.shape[0] // 2, *full.shape[1:])
        self.f32, self.bf16 = shape(half, F32), shape(half, BF16)
        self.total, self.low = call(
            scan_begin_kernel, (self.f32, self.bf16), after(full, *others), self.other
        )
        self.part = self.total

    def step(self, i, first=(), then=()):
        came = send(after(self.low, *first), SCAN[i])
        self.total, self.part, self.low = call(
            functools.partial(scan_kernel, i, self.reverse),
            (self.f32, self.f32, self.bf16),
            after(self.total, *then), self.part, came,
        )

    def end(self, *others):
        back = send(after(self.low, *others), SWAP)
        return call(
            functools.partial(scan_end_kernel, self.reverse),
            (shape(self.other.shape, BF16),),
            self.part, back, self.other,
        )[0]


def halves_kernel(a_ref, b_ref, lo_ref, hi_ref):
    rows = lo_ref.shape[0]
    lo_ref[...] = a_ref[:rows]
    hi_ref[...] = b_ref[rows:]


def chip_sums(own, came):
    _, width, cols = own.shape
    full, half = shape((4, width, cols), BF16), shape((2, width, cols), BF16)
    return call(chip_sum_kernel, (full, full, half, half, full), own, came)


def line_sums(own, *lines):
    _, width, cols = own.shape
    return call(line_sum_kernel, (shape((width, cols), BF16),) * 4, own, *lines)


def last_sum(lines, factor):
    width, cols = lines[0].shape
    kernel = functools.partial(last_sum_kernel, factor)
    return call(kernel, (shape((cols, width), F32),), *lines)[0]


def body(queries, keys, values, gain, out_weight, cotangent):
    tokens, width = queries.shape
    heads = width // DH
    state = shape((heads, DH, DH), F32)
    state_low = shape((heads, DH, DH), BF16)
    whole_f32 = shape((tokens, width), F32)
    whole_bf16 = shape((tokens, width), BF16)
    gain2 = gain.reshape(1, width)

    rows = out_weight.shape[0]
    came = [send(out_weight, ALONG_A[o]) for o in (1, 2, 3)]
    full, low = call(states_kernel, (state, state_low), keys, values)
    scan = Scan(False)
    scan.begin(full, low)
    scan.step(0)
    came[0] = after(came[0], scan.total)
    line = place(rows, 4 * rows, line_slots, (0,), [out_weight, *came])
    scan.step(1)
    before, behind = send(line, ALONG_B[1]), send(line, ALONG_B[3])
    scan.step(2)
    half_line = shape((2 * rows, width), BF16)
    lo, hi = call(halves_kernel, (half_line, half_line), before, behind)
    (intra,) = call(intra_kernel, (whole_f32,), after(queries, lo), keys, values)
    scan.step(3, (lo,), (intra,))
    far_lo, far_hi = send(lo, ALONG_B[1]), send(hi, ALONG_B[3])
    own = [line, before, behind, far_lo, far_hi]
    other = [send(piece, SWAP) for piece in own]
    prefix = scan.end(far_lo, far_hi)
    size = rows * NY * NX * NC
    weight = place(rows, size, functools.partial(gather_slots, False), (0, 3, 1, 2), own)
    weight = place(
        rows, size, functools.partial(gather_slots, True), (0, 3, 1, 2), other, into=weight
    )
    attended, normed, turned = call(
        normed_kernel,
        (whole_f32, whole_bf16, shape((width, tokens), BF16)),
        intra, queries, prefix, gain2,
    )

    long = ring_step(4, normed, weight)
    short = ring_step(-3, normed, weight)
    grad_normed = call(grad_normed_kernel, (whole_f32,), after(cotangent, long, short), weight)[0]
    grad_att, g_full, g_low = call(
        grad_att_kernel, (whole_bf16, state, state_low), grad_normed, attended, gain2, queries
    )
    scan = Scan(True)
    scan.begin(g_full, g_low)
    own, other = terms_of(cotangent, after(turned, scan.total))
    scan.step(0, (), (own,))

    came = send(long, LONG), send(short, SHORT)
    ready = after(normed, scan.total)
    long = ring_step(3, ready, weight, came[0], cost=LONGEST)
    short = ring_step(-2, ready, weight, came[1])
    came = send(after(other, long, short), SWAP)
    grad_queries, dk_part, dv_part = call(
        back_kernel,
        (whole_bf16, whole_f32, whole_f32),
        queries, keys, values, after(grad_att, long, short), prefix,
    )
    scan.step(1, (long, short), (dk_part,))
    here, up, far_lo, far_hi, down = chip_sums(after(own, scan.total), came)
    far = send(far_lo, ALONG_B[1]), send(far_hi, ALONG_B[3])
    scan.step(2, (), (here,))
    up, down = call(relay_kernel, (shape(up.shape, BF16),) * 2, up, down, *far)

    came = send(long, LONG), send(short, SHORT)
    ready = after(normed, scan.total, up)
    long = ring_step(2, ready, weight, came[0], cost=LONGEST)
    short = ring_step(-1, ready, weight, came[1])
    near = send(after(up, long, short), ALONG_B[1]), send(after(down, long, short), ALONG_B[3])
    scan.step(3, (long, short))
    line = line_sums(here, *near)

    came = send(long, LONG), send(short, SHORT)
    ready = after(normed, scan.part, line[0], came[1])
    long = ring_step(1, ready, weight, came[0])
    suffix = scan.end(long)
    grad_keys, grad_values = call(
        finish_kernel, (whole_bf16, whole_bf16), dk_part, dv_part, keys, values, suffix
    )
    last = [send(after(line[o], long), ALONG_A[o]) for o in (1, 3, 2)]
    grad_weight = last_sum([line[0], *last], (tokens * NY * NX * NC) ** -0.5)
    layer_out = ring_step(0, normed, weight, send(long, LONG), came[1])
    return (layer_out, grad_queries, grad_keys, grad_values, grad_weight)


def solution(mesh):
    placed = (
        P("seq", "head"),
        P("seq", "head"),
        P("seq", "head"),
        P("head"),
        P("seq", "head"),
        P("seq", None),
    )
    return jax.shard_map(
        body,
        mesh=mesh,
        in_specs=placed,
        out_specs=(P("seq", "head"),) * 5,
        check_vma=False,
    )
```

```python
import functools

import jax
import jax.numpy as jnp
from jax import lax
from jax.experimental import pallas as pl
from jax.experimental.pallas import tpu as pltpu
from jax.sharding import PartitionSpec as P

DH = 128
SPAN = 512
EPS = 1e-06
ROOM = 16 * 2**20
FREE = pl.CostEstimate(flops=0, bytes_accessed=0, transcendentals=0)
LONGEST = pl.CostEstimate(flops=2 * 10**10, bytes_accessed=0, transcendentals=0)
NY, NX, NC, NZ = 4, 4, 2, 8
AXES = ("seq", "head")
F32, BF16 = jnp.float32, jnp.bfloat16
NT = (((1,), (1,)), ((), ()))
NN = (((1,), (0,)), ((), ()))
TN = (((0,), (0,)), ((), ()))


def dot(a, b, dims):
    return lax.dot_general(a, b, dims, preferred_element_type=F32)


def pairs(move):
    out = []
    for y in range(NY):
        for x in range(NX):
            for c in range(NC):
                for z in range(NZ):
                    ty, tx, tc, tz = move(y, x, c, z)
                    here = ((y * NX + x) * NC + c) * NZ + z
                    there = (((ty % NY) * NX + tx % NX) * NC + tc) * NZ + tz % NZ
                    out.append((here, there))
    return out


SWAP = pairs(lambda y, x, c, z: (y, x, 1 - c, z))
SCAN = (
    pairs(lambda y, x, c, z: (y, x ^ 1, c, z)),
    pairs(lambda y, x, c, z: (y, 3 - x, c, z)),
    pairs(lambda y, x, c, z: (y ^ 1, x, c, z)),
    pairs(lambda y, x, c, z: (3 - y, x, c, z)),
)
ALONG_A = {
    o: pairs(lambda y, x, c, z, o=o: (y, x + o, c, z) if c == 0 else (y + o, x, c, z))
    for o in (1, 2, 3)
}
ALONG_B = {
    o: pairs(lambda y, x, c, z, o=o: (y + o, x, c, z) if c == 0 else (y, x + o, c, z))
    for o in (1, 2, 3)
}
LONG = pairs(lambda y, x, c, z: (y, x, c, z - 1 if c == 0 else z + 1))
SHORT = pairs(lambda y, x, c, z: (y, x, c, z + 1 if c == 0 else z - 1))


def send(value, perm):
    return lax.ppermute(value, AXES, perm)


def after(value, *others):
    return lax.optimization_barrier((value, *others))[0]


def whole(n):
    return [pl.BlockSpec(memory_space=pltpu.VMEM)] * n


def call(kernel, outs, *args, cost=FREE, **extra):
    return pl.pallas_call(
        kernel,
        out_shape=tuple(outs),
        in_specs=whole(len(args)),
        out_specs=tuple(whole(len(outs))),
        compiler_params=pltpu.CompilerParams(vmem_limit_bytes=ROOM),
        cost_estimate=cost,
        **extra,
    )(*args)


def place_of():
    s = lax.axis_index("seq")
    return s >> 3, (s >> 1) & 3, s & 1, lax.axis_index("head")


def shape(dims, dtype):
    return jax.ShapeDtypeStruct(dims, dtype)


def head(ref, h, rows=slice(None)):
    return ref[rows, h * DH : (h + 1) * DH]


def states_kernel(k_ref, v_ref, full_ref, sent_ref):
    for h in range(full_ref.shape[0]):
        state = dot(head(k_ref, h), head(v_ref, h), TN)
        full_ref[h] = state
        sent_ref[h] = state.astype(BF16)


def lower(n):
    return lax.broadcasted_iota(jnp.int32, (n, n), 0) >= lax.broadcasted_iota(jnp.int32, (n, n), 1)


HALF = SPAN // 2


def intra_kernel(q_ref, k_ref, v_ref, out_ref):
    keep = lower(HALF)
    lo, hi = slice(0, HALF), slice(HALF, SPAN)
    for h in range(q_ref.shape[1] // DH):
        k0, k1 = head(k_ref, h, lo), head(k_ref, h, hi)
        v0, v1 = head(v_ref, h, lo), head(v_ref, h, hi)
        q0, q1 = head(q_ref, h, lo), head(q_ref, h, hi)
        s00 = jnp.where(keep, dot(q0, k0, NT), 0.0).astype(BF16)
        s10 = dot(q1, k0, NT).astype(BF16)
        s11 = jnp.where(keep, dot(q1, k1, NT), 0.0).astype(BF16)
        out_ref[lo, h * DH : (h + 1) * DH] = dot(s00, v0, NN)
        out_ref[hi, h * DH : (h + 1) * DH] = dot(s10, v0, NN) + dot(s11, v1, NN)


def normed_kernel(intra_ref, q_ref, prefix_ref, gain_ref, att_ref, normed_ref, turned_ref):
    for h in range(q_ref.shape[1] // DH):
        cols = slice(h * DH, (h + 1) * DH)
        att = intra_ref[:, cols] + dot(q_ref[:, cols], prefix_ref[h], NN)
        att_ref[:, cols] = att
        inv = lax.rsqrt(jnp.mean(att * att, axis=-1, keepdims=True) + EPS)
        normed = (att * inv * gain_ref[:, cols]).astype(BF16)
        normed_ref[:, cols] = normed
        turned_ref[cols, :] = normed.T


def grad_att_kernel(gn_ref, att_ref, gain_ref, q_ref, g_ref, full_ref, sent_ref):
    for h in range(q_ref.shape[1] // DH):
        cols = slice(h * DH, (h + 1) * DH)
        att = att_ref[:, cols]
        inv = lax.rsqrt(jnp.mean(att * att, axis=-1, keepdims=True) + EPS)
        a = gn_ref[:, cols] * gain_ref[:, cols]
        inner = jnp.mean(a * att, axis=-1, keepdims=True)
        g = (inv * (a - att * (inv * inv * inner))).astype(BF16)
        g_ref[:, cols] = g
        state = dot(q_ref[:, cols], g, TN)
        full_ref[h] = state
        sent_ref[h] = state.astype(BF16)


def queries_kernel(k_ref, v_ref, g_ref, prefix_ref, dq_ref):
    keep = lower(HALF)
    lo, hi = slice(0, HALF), slice(HALF, SPAN)
    for h in range(k_ref.shape[1] // DH):
        cols = slice(h * DH, (h + 1) * DH)
        k0, k1 = k_ref[lo, cols], k_ref[hi, cols]
        v0, v1 = v_ref[lo, cols], v_ref[hi, cols]
        g0, g1 = g_ref[lo, cols], g_ref[hi, cols]
        prefix = prefix_ref[h]
        d00 = jnp.where(keep, dot(g0, v0, NT), 0.0).astype(BF16)
        d10 = dot(g1, v0, NT).astype(BF16)
        d11 = jnp.where(keep, dot(g1, v1, NT), 0.0).astype(BF16)
        dq_ref[lo, cols] = (dot(d00, k0, NN) + dot(g0, prefix, NT)).astype(BF16)
        dq_ref[hi, cols] = (dot(d10, k0, NN) + dot(d11, k1, NN) + dot(g1, prefix, NT)).astype(BF16)


def inner_kernel(q_ref, k_ref, v_ref, g_ref, dk_ref, dv_ref):
    upper = lax.broadcasted_iota(jnp.int32, (HALF, HALF), 0) <= lax.broadcasted_iota(
        jnp.int32, (HALF, HALF), 1
    )
    lo, hi = slice(0, HALF), slice(HALF, SPAN)
    for h in range(q_ref.shape[1] // DH):
        cols = slice(h * DH, (h + 1) * DH)
        q0, q1 = q_ref[lo, cols], q_ref[hi, cols]
        k0, k1 = k_ref[lo, cols], k_ref[hi, cols]
        v0, v1 = v_ref[lo, cols], v_ref[hi, cols]
        g0, g1 = g_ref[lo, cols], g_ref[hi, cols]
        e00 = jnp.where(upper, dot(v0, g0, NT), 0.0).astype(BF16)
        e01 = dot(v0, g1, NT).astype(BF16)
        e11 = jnp.where(upper, dot(v1, g1, NT), 0.0).astype(BF16)
        dk_ref[lo, cols] = dot(e00, q0, NN) + dot(e01, q1, NN)
        dk_ref[hi, cols] = dot(e11, q1, NN)
        s00 = jnp.where(upper, dot(k0, q0, NT), 0.0).astype(BF16)
        s01 = dot(k0, q1, NT).astype(BF16)
        s11 = jnp.where(upper, dot(k1, q1, NT), 0.0).astype(BF16)
        dv_ref[lo, cols] = dot(s00, g0, NN) + dot(s01, g1, NN)
        dv_ref[hi, cols] = dot(s11, g1, NN)


def finish_kernel(dk_part_ref, dv_part_ref, k_ref, v_ref, suffix_ref, dk_ref, dv_ref):
    for h in range(k_ref.shape[1] // DH):
        cols = slice(h * DH, (h + 1) * DH)
        suffix = suffix_ref[h]
        dk_ref[:, cols] = (dk_part_ref[:, cols] + dot(v_ref[:, cols], suffix, NT)).astype(BF16)
        dv_ref[:, cols] = (dv_part_ref[:, cols] + dot(k_ref[:, cols], suffix, NN)).astype(BF16)


def grad_normed_kernel(cot_ref, w_ref, out_ref):
    block = 1024

    def lap(i, _):
        at = pl.multiple_of(i * block, block)
        part = dot(cot_ref[:, pl.ds(at, block)], w_ref[pl.ds(at, block), :], NN)

        @pl.when(i == 0)
        def _():
            out_ref[...] = part

        @pl.when(i > 0)
        def _():
            out_ref[...] += part

        return 0

    lax.fori_loop(0, cot_ref.shape[1] // block, lap, 0)


def ring_kernel(away, normed_ref, w_ref, *refs):
    group = normed_ref.shape[1]
    _, _, core, z = place_of()
    owner = (z + jnp.where(core == 0, -away, away)) & (NZ - 1)
    rows = pl.ds(pl.multiple_of(owner * group, group), group)
    part = dot(normed_ref[...], w_ref[rows, :], NT)
    for came_ref in refs[:-1]:
        part = part + came_ref[...].astype(F32)
    refs[-1][...] = part.astype(BF16)


def ring_step(away, normed, weight, *came, cost=FREE):
    out = shape(normed.shape, BF16)
    kernel = functools.partial(ring_kernel, away)
    return call(kernel, (out,), normed, weight, *came, cost=cost)[0]


def chip_at(b, a, at):
    y, x, core, _ = at
    row = (y + jnp.where(core == 0, b, a)) & 3
    col = (x + jnp.where(core == 0, a, b)) & 3
    return row * NX + col


def terms_kernel(turned_ref, cot_ref, own_ref, other_ref):
    at = place_of()
    first = at[2] == 0
    cols = own_ref.shape[2]

    def lap(b, _):
        for a in range(4):
            start = pl.multiple_of(chip_at(b, a, at) * (NC * cols), NC * cols)
            res = dot(turned_ref[...], cot_ref[:, pl.ds(start, NC * cols)], NN).astype(BF16)
            lo, hi = res[:, :cols], res[:, cols:]
            own_ref[b * 4 + a] = jnp.where(first, lo, hi)
            other_ref[b * 4 + a] = jnp.where(first, hi, lo)
        return 0

    lax.fori_loop(0, 4, lap, 0)


def terms_of(cotangent, turned):
    chips = NY * NX
    half = shape((chips, turned.shape[0], cotangent.shape[1] // chips // NC), BF16)
    return call(terms_kernel, (half, half), turned, cotangent)


def chip_sum_kernel(own_ref, came_ref, here_ref, up_ref, far_lo_ref, far_hi_ref, down_ref):
    for b in range(4):
        for a in range(4):
            total = own_ref[b * 4 + a].astype(F32) + came_ref[a * 4 + b].astype(F32)
            total = total.astype(BF16)
            if b == 2:
                (far_lo_ref if a < 2 else far_hi_ref)[a % 2] = total
            else:
                (here_ref, up_ref, None, down_ref)[b][a] = total


def relay_kernel(up_ref, down_ref, lo_ref, hi_ref, up_out_ref, down_out_ref):
    for a in range(4):
        if a < 2:
            up_out_ref[a] = (up_ref[a].astype(F32) + lo_ref[a].astype(F32)).astype(BF16)
            down_out_ref[a] = down_ref[a]
        else:
            up_out_ref[a] = up_ref[a]
            down_out_ref[a] = (down_ref[a].astype(F32) + hi_ref[a - 2].astype(F32)).astype(BF16)


def line_sum_kernel(own_ref, *refs):
    came, outs = refs[:2], refs[2:]
    for a in range(4):
        total = own_ref[a].astype(F32)
        for ref in came:
            total = total + ref[a].astype(F32)
        outs[a][...] = total.astype(BF16)


def last_sum_kernel(factor, own_ref, a_ref, b_ref, c_ref, out_ref):
    total = own_ref[...].astype(F32)
    for ref in (a_ref, b_ref, c_ref):
        total = total + ref[...].astype(F32)
    out_ref[...] = total.T * factor


def line_slots(_):
    y, x, core, _ = place_of()
    here = jnp.where(core == 0, x, y)
    return [(here - o) & 3 for o in range(4)]


def gather_slots(other, b):
    y, x, core, _ = place_of()
    core = 1 - core if other else core
    out = []
    for a in range(4):
        row = jnp.where(core == 0, (y + b) & 3, a)
        col = jnp.where(core == 0, a, (x + b) & 3)
        out.append((row * NX + col) * NC + core)
    return out


def place_kernel(rows, counts, slots, lines, *refs):
    out_ref = refs[-1]
    places = [p for line in lines for p in slots(line)]
    n = 0
    for piece, count in zip(refs, counts):
        for i in range(count):
            to = pl.multiple_of(places[n] * rows, rows)
            out_ref[pl.ds(to, rows), :] = piece[i * rows : (i + 1) * rows, :]
            n += 1


def place(rows, total, slots, lines, pieces, into=None, cost=FREE):
    counts = tuple(p.shape[0] // rows for p in pieces)
    kernel = functools.partial(place_kernel, rows, counts, slots, lines)
    out = shape((total, pieces[0].shape[1]), BF16)
    if into is None:
        return call(kernel, (out,), *pieces, cost=cost)[0]
    return call(kernel, (out,), *pieces, into, input_output_aliases={len(pieces): 0})[0]


def scan_begin_kernel(full_ref, came_ref, total_ref, low_ref):
    half = total_ref.shape[0]
    first = place_of()[2] * half
    for h in range(half):
        total = full_ref[first + h] + came_ref[first + h].astype(F32)
        total_ref[h] = total
        low_ref[h] = total.astype(BF16)


def scan_kernel(step, reverse, total_ref, part_ref, came_ref, total_out, part_out, low_ref):
    line = place_of()[0 if step >= 2 else 1]
    behind = (line & 1) if step % 2 == 0 else line >> 1
    counts = (1 - behind if reverse else behind).astype(F32)
    for h in range(total_ref.shape[0]):
        came = came_ref[h].astype(F32)
        total = total_ref[h] + came
        total_out[h] = total
        part_out[h] = came * counts if step == 0 else part_ref[h] + came * counts
        low_ref[h] = (part_out[h] if step == 3 else total).astype(BF16)


def scan_end_kernel(reverse, part_ref, back_ref, other_ref, out_ref):
    half = part_ref.shape[0]
    core = place_of()[2]
    own = core * half
    counts = (1 - core if reverse else core).astype(F32)
    for h in range(half):
        other = other_ref[own + h].astype(F32) * counts
        out_ref[own + h] = (part_ref[h] + other).astype(BF16)
        other = other_ref[half - own + h].astype(F32) * counts
        out_ref[half - own + h] = (back_ref[h].astype(F32) + other).astype(BF16)


class Scan:

    def __init__(self, reverse):
        self.reverse = reverse

    def begin(self, full, low, *others):
        self.other = send(low, SWAP)
        half = (full.shape[0] // 2, *full.shape[1:])
        self.f32, self.bf16 = shape(half, F32), shape(half, BF16)
        self.total, self.low = call(
            scan_begin_kernel, (self.f32, self.bf16), after(full, *others), self.other
        )
        self.part = self.total

    def step(self, i, first=(), then=(), cost=FREE):
        came = send(after(self.low, *first), SCAN[i])
        self.total, self.part, self.low = call(
            functools.partial(scan_kernel, i, self.reverse),
            (self.f32, self.f32, self.bf16),
            after(self.total, *then), self.part, came,
            cost=cost,
        )

    def end(self, *others):
        back = send(after(self.low, *others), SWAP)
        return call(
            functools.partial(scan_end_kernel, self.reverse),
            (shape(self.other.shape, BF16),),
            self.part, back, self.other,
        )[0]


def halves_kernel(a_ref, b_ref, lo_ref, hi_ref):
    rows = lo_ref.shape[0]
    lo_ref[...] = a_ref[:rows]
    hi_ref[...] = b_ref[rows:]


def chip_sums(own, came):
    _, width, cols = own.shape
    full, half = shape((4, width, cols), BF16), shape((2, width, cols), BF16)
    return call(chip_sum_kernel, (full, full, half, half, full), own, came)


def line_sums(own, *lines):
    _, width, cols = own.shape
    return call(line_sum_kernel, (shape((width, cols), BF16),) * 4, own, *lines)


def last_sum(lines, factor):
    width, cols = lines[0].shape
    kernel = functools.partial(last_sum_kernel, factor)
    return call(kernel, (shape((cols, width), F32),), *lines)[0]


def body(queries, keys, values, gain, out_weight, cotangent):
    tokens, width = queries.shape
    heads = width // DH
    state = shape((heads, DH, DH), F32)
    state_low = shape((heads, DH, DH), BF16)
    whole_f32 = shape((tokens, width), F32)
    whole_bf16 = shape((tokens, width), BF16)
    gain2 = gain.reshape(1, width)

    rows = out_weight.shape[0]
    came = [send(out_weight, ALONG_A[o]) for o in (1, 2, 3)]
    full, low = call(states_kernel, (state, state_low), keys, values)
    scan = Scan(False)
    scan.begin(full, low, *came)
    line = place(rows, 4 * rows, line_slots, (0,), [out_weight, after(came[0], scan.low), *came[1:]])
    scan.step(0, cost=LONGEST)
    scan.step(1)
    before, behind = send(line, ALONG_B[1]), send(line, ALONG_B[3])
    (intra,) = call(intra_kernel, (whole_f32,), after(queries, line), keys, values)
    half_line = shape((2 * rows, width), BF16)
    lo, hi = call(halves_kernel, (half_line, half_line), before, behind)
    scan.step(2, (intra,), (lo,))
    scan.step(3, (lo,))
    far_lo, far_hi = send(lo, ALONG_B[1]), send(hi, ALONG_B[3])
    own = [line, before, behind, far_lo, far_hi]
    other = [send(piece, SWAP) for piece in own]
    prefix = scan.end(far_lo, far_hi)
    size = rows * NY * NX * NC
    weight = place(rows, size, functools.partial(gather_slots, False), (0, 3, 1, 2), own)
    weight = place(
        rows, size, functools.partial(gather_slots, True), (0, 3, 1, 2), other, into=weight
    )
    attended, normed, turned = call(
        normed_kernel,
        (whole_f32, whole_bf16, shape((width, tokens), BF16)),
        intra, queries, prefix, gain2,
    )

    long = ring_step(4, normed, weight)
    short = ring_step(-3, normed, weight)
    grad_normed = call(grad_normed_kernel, (whole_f32,), after(cotangent, long, short), weight)[0]
    grad_att, g_full, g_low = call(
        grad_att_kernel, (whole_bf16, state, state_low), grad_normed, attended, gain2, queries
    )
    scan = Scan(True)
    scan.begin(g_full, g_low)
    own, other = terms_of(cotangent, after(turned, scan.total))
    scan.step(0, (), (own,))

    came = send(long, LONG), send(short, SHORT)
    ready = after(normed, scan.total)
    long = ring_step(3, ready, weight, came[0], cost=LONGEST)
    short = ring_step(-2, ready, weight, came[1])
    here, up, far_lo, far_hi, down = chip_sums(own, send(other, SWAP))
    far = send(far_lo, ALONG_B[1]), send(far_hi, ALONG_B[3])
    dk_part, dv_part = call(
        inner_kernel, (whole_f32, whole_f32), queries, keys, values, after(grad_att, here)
    )
    scan.step(1, (long, short), (dk_part,))
    (grad_queries,) = call(
        queries_kernel, (whole_bf16,), keys, values, after(grad_att, scan.total), prefix
    )
    scan.step(2, (), (grad_queries,))
    up, down = call(relay_kernel, (shape(up.shape, BF16),) * 2, up, down, *far)

    came = send(long, LONG), send(short, SHORT)
    ready = after(normed, scan.total, up)
    long = ring_step(2, ready, weight, came[0], cost=LONGEST)
    short = ring_step(-1, ready, weight, came[1])
    near = send(after(up, long, short), ALONG_B[1]), send(after(down, long, short), ALONG_B[3])
    scan.step(3, (long, short))

    came = send(long, LONG), send(short, SHORT)
    suffix = scan.end()
    grad_keys, grad_values = call(
        finish_kernel, (whole_bf16, whole_bf16), dk_part, dv_part, keys, values, suffix
    )
    ready = after(normed, grad_keys, came[1])
    long = ring_step(1, ready, weight, came[0])
    line = line_sums(after(here, long), *near)
    last = [send(line[o], ALONG_A[o]) for o in (2, 1, 3)]
    layer_out = ring_step(0, normed, weight, send(long, LONG), came[1])
    here = after(line[0], layer_out)
    grad_weight = last_sum([here, *last], (tokens * NY * NX * NC) ** -0.5)
    return (layer_out, grad_queries, grad_keys, grad_values, grad_weight)


def solution(mesh):
    placed = (
        P("seq", "head"),
        P("seq", "head"),
        P("seq", "head"),
        P("head"),
        P("seq", "head"),
        P("seq", None),
    )
    return jax.shard_map(
        body,
        mesh=mesh,
        in_specs=placed,
        out_specs=(P("seq", "head"),) * 5,
        check_vma=False,
    )
```

```python
import functools

import jax
import jax.numpy as jnp
from jax import lax
from jax.experimental import pallas as pl
from jax.experimental.pallas import tpu as pltpu
from jax.sharding import PartitionSpec as P

DH = 128
SPAN = 512
EPS = 1e-06
ROOM = 16 * 2**20
FREE = pl.CostEstimate(flops=0, bytes_accessed=0, transcendentals=0)
LONGEST = pl.CostEstimate(flops=2 * 10**10, bytes_accessed=0, transcendentals=0)
NY, NX, NC, NZ = 4, 4, 2, 8
AXES = ("seq", "head")
F32, BF16 = jnp.float32, jnp.bfloat16
NT = (((1,), (1,)), ((), ()))
NN = (((1,), (0,)), ((), ()))
TN = (((0,), (0,)), ((), ()))


def dot(a, b, dims):
    return lax.dot_general(a, b, dims, preferred_element_type=F32)


def pairs(move):
    out = []
    for y in range(NY):
        for x in range(NX):
            for c in range(NC):
                for z in range(NZ):
                    ty, tx, tc, tz = move(y, x, c, z)
                    here = ((y * NX + x) * NC + c) * NZ + z
                    there = (((ty % NY) * NX + tx % NX) * NC + tc) * NZ + tz % NZ
                    out.append((here, there))
    return out


SWAP = pairs(lambda y, x, c, z: (y, x, 1 - c, z))
SCAN = (
    pairs(lambda y, x, c, z: (y, x ^ 1, c, z)),
    pairs(lambda y, x, c, z: (y, 3 - x, c, z)),
    pairs(lambda y, x, c, z: (y ^ 1, x, c, z)),
    pairs(lambda y, x, c, z: (3 - y, x, c, z)),
)
ALONG_A = {
    o: pairs(lambda y, x, c, z, o=o: (y, x + o, c, z) if c == 0 else (y + o, x, c, z))
    for o in (1, 2, 3)
}
ALONG_B = {
    o: pairs(lambda y, x, c, z, o=o: (y + o, x, c, z) if c == 0 else (y, x + o, c, z))
    for o in (1, 2, 3)
}
LONG = pairs(lambda y, x, c, z: (y, x, c, z - 1 if c == 0 else z + 1))
SHORT = pairs(lambda y, x, c, z: (y, x, c, z + 1 if c == 0 else z - 1))


def send(value, perm):
    return lax.ppermute(value, AXES, perm)


def after(value, *others):
    return lax.optimization_barrier((value, *others))[0]


def whole(n):
    return [pl.BlockSpec(memory_space=pltpu.VMEM)] * n


def call(kernel, outs, *args, cost=FREE, **extra):
    return pl.pallas_call(
        kernel,
        out_shape=tuple(outs),
        in_specs=whole(len(args)),
        out_specs=tuple(whole(len(outs))),
        compiler_params=pltpu.CompilerParams(vmem_limit_bytes=ROOM),
        cost_estimate=cost,
        **extra,
    )(*args)


def place_of():
    s = lax.axis_index("seq")
    return s >> 3, (s >> 1) & 3, s & 1, lax.axis_index("head")


def shape(dims, dtype):
    return jax.ShapeDtypeStruct(dims, dtype)


def head(ref, h, rows=slice(None)):
    return ref[rows, h * DH : (h + 1) * DH]


def states_kernel(k_ref, v_ref, w_ref, full_ref, sent_ref, w_out_ref):
    w_out_ref[...] = w_ref[...]
    for h in range(full_ref.shape[0]):
        state = dot(head(k_ref, h), head(v_ref, h), TN)
        full_ref[h] = state
        sent_ref[h] = state.astype(BF16)


def lower(n):
    return lax.broadcasted_iota(jnp.int32, (n, n), 0) >= lax.broadcasted_iota(jnp.int32, (n, n), 1)


HALF = SPAN // 2


def intra_kernel(q_ref, k_ref, v_ref, out_ref):
    keep = lower(HALF)
    lo, hi = slice(0, HALF), slice(HALF, SPAN)
    for h in range(q_ref.shape[1] // DH):
        k0, k1 = head(k_ref, h, lo), head(k_ref, h, hi)
        v0, v1 = head(v_ref, h, lo), head(v_ref, h, hi)
        q0, q1 = head(q_ref, h, lo), head(q_ref, h, hi)
        s00 = jnp.where(keep, dot(q0, k0, NT), 0.0).astype(BF16)
        s10 = dot(q1, k0, NT).astype(BF16)
        s11 = jnp.where(keep, dot(q1, k1, NT), 0.0).astype(BF16)
        out_ref[lo, h * DH : (h + 1) * DH] = dot(s00, v0, NN)
        out_ref[hi, h * DH : (h + 1) * DH] = dot(s10, v0, NN) + dot(s11, v1, NN)


def normed_kernel(intra_ref, q_ref, prefix_ref, gain_ref, att_ref, normed_ref, turned_ref):
    for h in range(q_ref.shape[1] // DH):
        cols = slice(h * DH, (h + 1) * DH)
        att = intra_ref[:, cols] + dot(q_ref[:, cols], prefix_ref[h], NN)
        att_ref[:, cols] = att
        inv = lax.rsqrt(jnp.mean(att * att, axis=-1, keepdims=True) + EPS)
        normed = (att * inv * gain_ref[:, cols]).astype(BF16)
        normed_ref[:, cols] = normed
        turned_ref[cols, :] = normed.T


def grad_att_kernel(gn_ref, att_ref, gain_ref, q_ref, g_ref, full_ref, sent_ref):
    for h in range(q_ref.shape[1] // DH):
        cols = slice(h * DH, (h + 1) * DH)
        att = att_ref[:, cols]
        inv = lax.rsqrt(jnp.mean(att * att, axis=-1, keepdims=True) + EPS)
        a = gn_ref[:, cols] * gain_ref[:, cols]
        inner = jnp.mean(a * att, axis=-1, keepdims=True)
        g = (inv * (a - att * (inv * inv * inner))).astype(BF16)
        g_ref[:, cols] = g
        state = dot(q_ref[:, cols], g, TN)
        full_ref[h] = state
        sent_ref[h] = state.astype(BF16)


def queries_kernel(k_ref, v_ref, g_ref, prefix_ref, dq_ref):
    keep = lower(HALF)
    lo, hi = slice(0, HALF), slice(HALF, SPAN)
    for h in range(k_ref.shape[1] // DH):
        cols = slice(h * DH, (h + 1) * DH)
        k0, k1 = k_ref[lo, cols], k_ref[hi, cols]
        v0, v1 = v_ref[lo, cols], v_ref[hi, cols]
        g0, g1 = g_ref[lo, cols], g_ref[hi, cols]
        prefix = prefix_ref[h]
        d00 = jnp.where(keep, dot(g0, v0, NT), 0.0).astype(BF16)
        d10 = dot(g1, v0, NT).astype(BF16)
        d11 = jnp.where(keep, dot(g1, v1, NT), 0.0).astype(BF16)
        dq_ref[lo, cols] = (dot(d00, k0, NN) + dot(g0, prefix, NT)).astype(BF16)
        dq_ref[hi, cols] = (dot(d10, k0, NN) + dot(d11, k1, NN) + dot(g1, prefix, NT)).astype(BF16)


def inner_kernel(q_ref, k_ref, v_ref, g_ref, dk_ref, dv_ref):
    upper = lax.broadcasted_iota(jnp.int32, (HALF, HALF), 0) <= lax.broadcasted_iota(
        jnp.int32, (HALF, HALF), 1
    )
    lo, hi = slice(0, HALF), slice(HALF, SPAN)
    for h in range(q_ref.shape[1] // DH):
        cols = slice(h * DH, (h + 1) * DH)
        q0, q1 = q_ref[lo, cols], q_ref[hi, cols]
        k0, k1 = k_ref[lo, cols], k_ref[hi, cols]
        v0, v1 = v_ref[lo, cols], v_ref[hi, cols]
        g0, g1 = g_ref[lo, cols], g_ref[hi, cols]
        e00 = jnp.where(upper, dot(v0, g0, NT), 0.0).astype(BF16)
        e01 = dot(v0, g1, NT).astype(BF16)
        e11 = jnp.where(upper, dot(v1, g1, NT), 0.0).astype(BF16)
        dk_ref[lo, cols] = dot(e00, q0, NN) + dot(e01, q1, NN)
        dk_ref[hi, cols] = dot(e11, q1, NN)
        s00 = jnp.where(upper, dot(k0, q0, NT), 0.0).astype(BF16)
        s01 = dot(k0, q1, NT).astype(BF16)
        s11 = jnp.where(upper, dot(k1, q1, NT), 0.0).astype(BF16)
        dv_ref[lo, cols] = dot(s00, g0, NN) + dot(s01, g1, NN)
        dv_ref[hi, cols] = dot(s11, g1, NN)


def finish_kernel(dk_part_ref, dv_part_ref, k_ref, v_ref, suffix_ref, dk_ref, dv_ref):
    for h in range(k_ref.shape[1] // DH):
        cols = slice(h * DH, (h + 1) * DH)
        suffix = suffix_ref[h]
        dk_ref[:, cols] = (dk_part_ref[:, cols] + dot(v_ref[:, cols], suffix, NT)).astype(BF16)
        dv_ref[:, cols] = (dv_part_ref[:, cols] + dot(k_ref[:, cols], suffix, NN)).astype(BF16)


def grad_normed_kernel(cot_ref, w_ref, out_ref):
    block = 1024

    def lap(i, _):
        at = pl.multiple_of(i * block, block)
        part = dot(cot_ref[:, pl.ds(at, block)], w_ref[pl.ds(at, block), :], NN)

        @pl.when(i == 0)
        def _():
            out_ref[...] = part

        @pl.when(i > 0)
        def _():
            out_ref[...] += part

        return 0

    lax.fori_loop(0, cot_ref.shape[1] // block, lap, 0)


def ring_kernel(away, normed_ref, w_ref, *refs):
    group = normed_ref.shape[1]
    _, _, core, z = place_of()
    owner = (z + jnp.where(core == 0, -away, away)) & (NZ - 1)
    rows = pl.ds(pl.multiple_of(owner * group, group), group)
    part = dot(normed_ref[...], w_ref[rows, :], NT)
    for came_ref in refs[:-1]:
        part = part + came_ref[...].astype(F32)
    refs[-1][...] = part.astype(BF16)


def ring_step(away, normed, weight, *came, cost=FREE):
    out = shape(normed.shape, BF16)
    kernel = functools.partial(ring_kernel, away)
    return call(kernel, (out,), normed, weight, *came, cost=cost)[0]


def chip_at(b, a, at):
    y, x, core, _ = at
    row = (y + jnp.where(core == 0, b, a)) & 3
    col = (x + jnp.where(core == 0, a, b)) & 3
    return row * NX + col


def terms_kernel(turned_ref, cot_ref, own_ref, other_ref):
    at = place_of()
    first = at[2] == 0
    cols = own_ref.shape[2]

    def lap(b, _):
        for a in range(4):
            start = pl.multiple_of(chip_at(b, a, at) * (NC * cols), NC * cols)
            res = dot(turned_ref[...], cot_ref[:, pl.ds(start, NC * cols)], NN).astype(BF16)
            lo, hi = res[:, :cols], res[:, cols:]
            own_ref[b * 4 + a] = jnp.where(first, lo, hi)
            other_ref[b * 4 + a] = jnp.where(first, hi, lo)
        return 0

    lax.fori_loop(0, 4, lap, 0)


def terms_of(cotangent, turned):
    chips = NY * NX
    half = shape((chips, turned.shape[0], cotangent.shape[1] // chips // NC), BF16)
    return call(terms_kernel, (half, half), turned, cotangent)


def chip_sum_kernel(own_ref, came_ref, here_ref, up_ref, far_lo_ref, far_hi_ref, down_ref):
    for b in range(4):
        for a in range(4):
            total = own_ref[b * 4 + a].astype(F32) + came_ref[a * 4 + b].astype(F32)
            total = total.astype(BF16)
            if b == 2:
                (far_lo_ref if a < 2 else far_hi_ref)[a % 2] = total
            else:
                (here_ref, up_ref, None, down_ref)[b][a] = total


def relay_kernel(up_ref, down_ref, lo_ref, hi_ref, up_out_ref, down_out_ref):
    for a in range(4):
        if a < 2:
            up_out_ref[a] = (up_ref[a].astype(F32) + lo_ref[a].astype(F32)).astype(BF16)
            down_out_ref[a] = down_ref[a]
        else:
            up_out_ref[a] = up_ref[a]
            down_out_ref[a] = (down_ref[a].astype(F32) + hi_ref[a - 2].astype(F32)).astype(BF16)


def line_sum_kernel(own_ref, *refs):
    came, outs = refs[:2], refs[2:]
    for a in range(4):
        total = own_ref[a].astype(F32)
        for ref in came:
            total = total + ref[a].astype(F32)
        outs[a][...] = total.astype(BF16)


def last_sum_kernel(factor, own_ref, a_ref, b_ref, c_ref, out_ref):
    total = own_ref[...].astype(F32)
    for ref in (a_ref, b_ref, c_ref):
        total = total + ref[...].astype(F32)
    out_ref[...] = total.T * factor


def line_slots(_):
    y, x, core, _ = place_of()
    here = jnp.where(core == 0, x, y)
    return [(here - o) & 3 for o in range(4)]


def gather_slots(other, b):
    y, x, core, _ = place_of()
    core = 1 - core if other else core
    out = []
    for a in range(4):
        row = jnp.where(core == 0, (y + b) & 3, a)
        col = jnp.where(core == 0, a, (x + b) & 3)
        out.append((row * NX + col) * NC + core)
    return out


def place_kernel(rows, counts, slots, lines, *refs):
    out_ref = refs[-1]
    places = [p for line in lines for p in slots(line)]
    n = 0
    for piece, count in zip(refs, counts):
        for i in range(count):
            to = pl.multiple_of(places[n] * rows, rows)
            out_ref[pl.ds(to, rows), :] = piece[i * rows : (i + 1) * rows, :]
            n += 1


def place(rows, total, slots, lines, pieces, into=None, cost=FREE):
    counts = tuple(p.shape[0] // rows for p in pieces)
    kernel = functools.partial(place_kernel, rows, counts, slots, lines)
    out = shape((total, pieces[0].shape[1]), BF16)
    if into is None:
        return call(kernel, (out,), *pieces, cost=cost)[0]
    return call(kernel, (out,), *pieces, into, input_output_aliases={len(pieces): 0})[0]


def scan_begin_kernel(full_ref, came_ref, total_ref, low_ref):
    half = total_ref.shape[0]
    first = place_of()[2] * half
    for h in range(half):
        total = full_ref[first + h] + came_ref[first + h].astype(F32)
        total_ref[h] = total
        low_ref[h] = total.astype(BF16)


def scan_kernel(step, reverse, total_ref, part_ref, came_ref, *outs):
    line = place_of()[0 if step >= 2 else 1]
    behind = (line & 1) if step % 2 == 0 else line >> 1
    counts = (1 - behind if reverse else behind).astype(F32)
    part_out, low_ref = outs[:2]
    for h in range(total_ref.shape[0]):
        came = came_ref[h].astype(F32)
        part = came * counts if step == 0 else part_ref[h] + came * counts
        part_out[h] = part
        if step == 3:
            low_ref[h] = part.astype(BF16)
        else:
            total = total_ref[h] + came
            outs[2][h] = total
            low_ref[h] = total.astype(BF16)


def scan_end_kernel(reverse, part_ref, back_ref, other_ref, out_ref):
    half = part_ref.shape[0]
    core = place_of()[2]
    own = core * half
    counts = (1 - core if reverse else core).astype(F32)
    for h in range(half):
        other = other_ref[own + h].astype(F32) * counts
        out_ref[own + h] = (part_ref[h] + other).astype(BF16)
        other = other_ref[half - own + h].astype(F32) * counts
        out_ref[half - own + h] = (back_ref[h].astype(F32) + other).astype(BF16)


class Scan:

    def __init__(self, reverse):
        self.reverse = reverse

    def begin(self, full, low, *others):
        self.other = send(low, SWAP)
        half = (full.shape[0] // 2, *full.shape[1:])
        self.f32, self.bf16 = shape(half, F32), shape(half, BF16)
        self.total, self.low = call(
            scan_begin_kernel, (self.f32, self.bf16), after(full, *others), self.other
        )
        self.part = self.total

    def step(self, i, first=(), then=(), cost=FREE):
        came = send(after(self.low, *first), SCAN[i])
        outs = (self.f32, self.bf16) + ((self.f32,) if i < 3 else ())
        self.part, self.low, *total = call(
            functools.partial(scan_kernel, i, self.reverse),
            outs,
            after(self.total, *then), self.part, came,
            cost=cost,
        )
        self.total = total[0] if total else None

    def end(self, *others):
        back = send(after(self.low, *others), SWAP)
        return call(
            functools.partial(scan_end_kernel, self.reverse),
            (shape(self.other.shape, BF16),),
            self.part, back, self.other,
        )[0]


def halves_kernel(a_ref, b_ref, lo_ref, hi_ref):
    rows = lo_ref.shape[0]
    lo_ref[...] = a_ref[:rows]
    hi_ref[...] = b_ref[rows:]


def chip_sums(own, came):
    _, width, cols = own.shape
    full, half = shape((4, width, cols), BF16), shape((2, width, cols), BF16)
    return call(chip_sum_kernel, (full, full, half, half, full), own, came)


def line_sums(own, *lines):
    _, width, cols = own.shape
    return call(line_sum_kernel, (shape((width, cols), BF16),) * 4, own, *lines)


def last_sum(lines, factor):
    width, cols = lines[0].shape
    kernel = functools.partial(last_sum_kernel, factor)
    return call(kernel, (shape((cols, width), F32),), *lines)[0]


def body(queries, keys, values, gain, out_weight, cotangent):
    tokens, width = queries.shape
    heads = width // DH
    state = shape((heads, DH, DH), F32)
    state_low = shape((heads, DH, DH), BF16)
    whole_f32 = shape((tokens, width), F32)
    whole_bf16 = shape((tokens, width), BF16)
    gain2 = gain.reshape(1, width)

    rows = out_weight.shape[0]
    came = [send(out_weight, ALONG_A[o]) for o in (1, 2, 3)]
    block = shape(out_weight.shape, BF16)
    full, low, block = call(states_kernel, (state, state_low, block), keys, values, out_weight)
    scan = Scan(False)
    scan.begin(full, low, *came)
    line = place(rows, 4 * rows, line_slots, (0,), [block, after(came[0], scan.low), *came[1:]])
    scan.step(0, cost=LONGEST)
    scan.step(1)
    before, behind = send(line, ALONG_B[1]), send(line, ALONG_B[3])
    (intra,) = call(intra_kernel, (whole_f32,), after(queries, line), keys, values)
    half_line = shape((2 * rows, width), BF16)
    lo, hi = call(halves_kernel, (half_line, half_line), before, behind)
    scan.step(2, (intra,), (lo,))
    scan.step(3, (lo,))
    far_lo, far_hi = send(lo, ALONG_B[1]), send(hi, ALONG_B[3])
    own = [line, before, behind, far_lo, far_hi]
    other = [send(piece, SWAP) for piece in own]
    prefix = scan.end(far_lo, far_hi)
    size = rows * NY * NX * NC
    weight = place(rows, size, functools.partial(gather_slots, False), (0, 3, 1, 2), own)
    weight = place(
        rows, size, functools.partial(gather_slots, True), (0, 3, 1, 2), other, into=weight
    )
    attended, normed, turned = call(
        normed_kernel,
        (whole_f32, whole_bf16, shape((width, tokens), BF16)),
        intra, queries, prefix, gain2,
    )

    long = ring_step(4, normed, weight)
    short = ring_step(-3, normed, weight)
    grad_normed = call(grad_normed_kernel, (whole_f32,), after(cotangent, long, short), weight)[0]
    grad_att, g_full, g_low = call(
        grad_att_kernel, (whole_bf16, state, state_low), grad_normed, attended, gain2, queries
    )
    scan = Scan(True)
    scan.begin(g_full, g_low)
    own, other = terms_of(cotangent, after(turned, scan.total))
    scan.step(0, (), (own,))

    came = send(long, LONG), send(short, SHORT)
    ready = after(normed, scan.total)
    long = ring_step(3, ready, weight, came[0], cost=LONGEST)
    short = ring_step(-2, ready, weight, came[1])
    here, up, far_lo, far_hi, down = chip_sums(own, send(other, SWAP))
    far = send(far_lo, ALONG_B[1]), send(far_hi, ALONG_B[3])
    dk_part, dv_part = call(
        inner_kernel, (whole_f32, whole_f32), queries, keys, values, after(grad_att, here)
    )
    scan.step(1, (long, short), (dk_part,))
    (grad_queries,) = call(
        queries_kernel, (whole_bf16,), keys, values, after(grad_att, scan.total), prefix
    )
    scan.step(2, (), (grad_queries,))
    up, down = call(relay_kernel, (shape(up.shape, BF16),) * 2, up, down, *far)

    came = send(long, LONG), send(short, SHORT)
    ready = after(normed, scan.total, up)
    long = ring_step(2, ready, weight, came[0], cost=LONGEST)
    short = ring_step(-1, ready, weight, came[1])
    near = send(after(up, long, short), ALONG_B[1]), send(after(down, long, short), ALONG_B[3])
    scan.step(3, (long, short))

    came = send(long, LONG), send(short, SHORT)
    suffix = scan.end()
    grad_keys, grad_values = call(
        finish_kernel, (whole_bf16, whole_bf16), dk_part, dv_part, keys, values, suffix
    )
    ready = after(normed, grad_keys, came[1])
    long = ring_step(1, ready, weight, came[0])
    line = line_sums(after(here, long), *near)
    last = [send(line[o], ALONG_A[o]) for o in (2, 1, 3)]
    layer_out = ring_step(0, normed, weight, send(long, LONG), came[1])
    here = after(line[0], layer_out)
    grad_weight = last_sum([here, *last], (tokens * NY * NX * NC) ** -0.5)
    return (layer_out, grad_queries, grad_keys, grad_values, grad_weight)


def solution(mesh):
    placed = (
        P("seq", "head"),
        P("seq", "head"),
        P("seq", "head"),
        P("head"),
        P("seq", "head"),
        P("seq", None),
    )
    return jax.shard_map(
        body,
        mesh=mesh,
        in_specs=placed,
        out_specs=(P("seq", "head"),) * 5,
        check_vma=False,
    )
```

```python
import functools

import jax
import jax.numpy as jnp
from jax import lax
from jax.experimental import pallas as pl
from jax.experimental.pallas import tpu as pltpu
from jax.sharding import PartitionSpec as P

DH = 128
SPAN = 512
EPS = 1e-06
ROOM = 16 * 2**20
FREE = pl.CostEstimate(flops=0, bytes_accessed=0, transcendentals=0)
LONGEST = pl.CostEstimate(flops=2 * 10**10, bytes_accessed=0, transcendentals=0)
NY, NX, NC, NZ = 4, 4, 2, 8
AXES = ("seq", "head")
F32, BF16 = jnp.float32, jnp.bfloat16
NT = (((1,), (1,)), ((), ()))
NN = (((1,), (0,)), ((), ()))
TN = (((0,), (0,)), ((), ()))


def dot(a, b, dims):
    return lax.dot_general(a, b, dims, preferred_element_type=F32)


def pairs(move):
    out = []
    for y in range(NY):
        for x in range(NX):
            for c in range(NC):
                for z in range(NZ):
                    ty, tx, tc, tz = move(y, x, c, z)
                    here = ((y * NX + x) * NC + c) * NZ + z
                    there = (((ty % NY) * NX + tx % NX) * NC + tc) * NZ + tz % NZ
                    out.append((here, there))
    return out


SWAP = pairs(lambda y, x, c, z: (y, x, 1 - c, z))
SCAN = (
    pairs(lambda y, x, c, z: (y, x ^ 1, c, z)),
    pairs(lambda y, x, c, z: (y, 3 - x, c, z)),
    pairs(lambda y, x, c, z: (y ^ 1, x, c, z)),
    pairs(lambda y, x, c, z: (3 - y, x, c, z)),
)
ALONG_A = {
    o: pairs(lambda y, x, c, z, o=o: (y, x + o, c, z) if c == 0 else (y + o, x, c, z))
    for o in (1, 2, 3)
}
ALONG_B = {
    o: pairs(lambda y, x, c, z, o=o: (y + o, x, c, z) if c == 0 else (y, x + o, c, z))
    for o in (1, 2, 3)
}
LONG = pairs(lambda y, x, c, z: (y, x, c, z - 1 if c == 0 else z + 1))
SHORT = pairs(lambda y, x, c, z: (y, x, c, z + 1 if c == 0 else z - 1))


def send(value, perm):
    return lax.ppermute(value, AXES, perm)


def after(value, *others):
    return lax.optimization_barrier((value, *others))[0]


def whole(n):
    return [pl.BlockSpec(memory_space=pltpu.VMEM)] * n


def call(kernel, outs, *args, cost=FREE, **extra):
    return pl.pallas_call(
        kernel,
        out_shape=tuple(outs),
        in_specs=whole(len(args)),
        out_specs=tuple(whole(len(outs))),
        compiler_params=pltpu.CompilerParams(vmem_limit_bytes=ROOM),
        cost_estimate=cost,
        **extra,
    )(*args)


def place_of():
    s = lax.axis_index("seq")
    return s >> 3, (s >> 1) & 3, s & 1, lax.axis_index("head")


def shape(dims, dtype):
    return jax.ShapeDtypeStruct(dims, dtype)


def head(ref, h, rows=slice(None)):
    return ref[rows, h * DH : (h + 1) * DH]


def states_kernel(k_ref, v_ref, w_ref, full_ref, sent_ref, w_out_ref):
    w_out_ref[...] = w_ref[...]
    for h in range(full_ref.shape[0]):
        state = dot(head(k_ref, h), head(v_ref, h), TN)
        full_ref[h] = state
        sent_ref[h] = state.astype(BF16)


def lower(n):
    return lax.broadcasted_iota(jnp.int32, (n, n), 0) >= lax.broadcasted_iota(jnp.int32, (n, n), 1)


HALF = SPAN // 2


def intra_kernel(q_ref, k_ref, v_ref, out_ref):
    keep = lower(HALF)
    lo, hi = slice(0, HALF), slice(HALF, SPAN)
    for h in range(q_ref.shape[1] // DH):
        k0, k1 = head(k_ref, h, lo), head(k_ref, h, hi)
        v0, v1 = head(v_ref, h, lo), head(v_ref, h, hi)
        q0, q1 = head(q_ref, h, lo), head(q_ref, h, hi)
        s00 = jnp.where(keep, dot(q0, k0, NT), 0.0).astype(BF16)
        s10 = dot(q1, k0, NT).astype(BF16)
        s11 = jnp.where(keep, dot(q1, k1, NT), 0.0).astype(BF16)
        out_ref[lo, h * DH : (h + 1) * DH] = dot(s00, v0, NN)
        out_ref[hi, h * DH : (h + 1) * DH] = dot(s10, v0, NN) + dot(s11, v1, NN)


def normed_kernel(intra_ref, q_ref, prefix_ref, gain_ref, att_ref, normed_ref, turned_ref):
    for h in range(q_ref.shape[1] // DH):
        cols = slice(h * DH, (h + 1) * DH)
        att = intra_ref[:, cols] + dot(q_ref[:, cols], prefix_ref[h], NN)
        att_ref[:, cols] = att
        inv = lax.rsqrt(jnp.mean(att * att, axis=-1, keepdims=True) + EPS)
        normed = (att * inv * gain_ref[:, cols]).astype(BF16)
        normed_ref[:, cols] = normed
        turned_ref[cols, :] = normed.T


def grad_att_kernel(gn_ref, att_ref, gain_ref, q_ref, g_ref, full_ref, sent_ref):
    for h in range(q_ref.shape[1] // DH):
        cols = slice(h * DH, (h + 1) * DH)
        att = att_ref[:, cols]
        inv = lax.rsqrt(jnp.mean(att * att, axis=-1, keepdims=True) + EPS)
        a = gn_ref[:, cols] * gain_ref[:, cols]
        inner = jnp.mean(a * att, axis=-1, keepdims=True)
        g = (inv * (a - att * (inv * inv * inner))).astype(BF16)
        g_ref[:, cols] = g
        state = dot(q_ref[:, cols], g, TN)
        full_ref[h] = state
        sent_ref[h] = state.astype(BF16)


def queries_kernel(k_ref, v_ref, g_ref, prefix_ref, dq_ref):
    keep = lower(HALF)
    lo, hi = slice(0, HALF), slice(HALF, SPAN)
    for h in range(k_ref.shape[1] // DH):
        cols = slice(h * DH, (h + 1) * DH)
        k0, k1 = k_ref[lo, cols], k_ref[hi, cols]
        v0, v1 = v_ref[lo, cols], v_ref[hi, cols]
        g0, g1 = g_ref[lo, cols], g_ref[hi, cols]
        prefix = prefix_ref[h]
        d00 = jnp.where(keep, dot(g0, v0, NT), 0.0).astype(BF16)
        d10 = dot(g1, v0, NT).astype(BF16)
        d11 = jnp.where(keep, dot(g1, v1, NT), 0.0).astype(BF16)
        dq_ref[lo, cols] = (dot(d00, k0, NN) + dot(g0, prefix, NT)).astype(BF16)
        dq_ref[hi, cols] = (dot(d10, k0, NN) + dot(d11, k1, NN) + dot(g1, prefix, NT)).astype(BF16)


def inner_kernel(q_ref, k_ref, v_ref, g_ref, dk_ref, dv_ref):
    upper = lax.broadcasted_iota(jnp.int32, (HALF, HALF), 0) <= lax.broadcasted_iota(
        jnp.int32, (HALF, HALF), 1
    )
    lo, hi = slice(0, HALF), slice(HALF, SPAN)
    for h in range(q_ref.shape[1] // DH):
        cols = slice(h * DH, (h + 1) * DH)
        q0, q1 = q_ref[lo, cols], q_ref[hi, cols]
        k0, k1 = k_ref[lo, cols], k_ref[hi, cols]
        v0, v1 = v_ref[lo, cols], v_ref[hi, cols]
        g0, g1 = g_ref[lo, cols], g_ref[hi, cols]
        e00 = jnp.where(upper, dot(v0, g0, NT), 0.0).astype(BF16)
        e01 = dot(v0, g1, NT).astype(BF16)
        e11 = jnp.where(upper, dot(v1, g1, NT), 0.0).astype(BF16)
        dk_ref[lo, cols] = dot(e00, q0, NN) + dot(e01, q1, NN)
        dk_ref[hi, cols] = dot(e11, q1, NN)
        s00 = jnp.where(upper, dot(k0, q0, NT), 0.0).astype(BF16)
        s01 = dot(k0, q1, NT).astype(BF16)
        s11 = jnp.where(upper, dot(k1, q1, NT), 0.0).astype(BF16)
        dv_ref[lo, cols] = dot(s00, g0, NN) + dot(s01, g1, NN)
        dv_ref[hi, cols] = dot(s11, g1, NN)


def finish_kernel(dk_part_ref, dv_part_ref, k_ref, v_ref, suffix_ref, dk_ref, dv_ref):
    for h in range(k_ref.shape[1] // DH):
        cols = slice(h * DH, (h + 1) * DH)
        suffix = suffix_ref[h]
        dk_ref[:, cols] = (dk_part_ref[:, cols] + dot(v_ref[:, cols], suffix, NT)).astype(BF16)
        dv_ref[:, cols] = (dv_part_ref[:, cols] + dot(k_ref[:, cols], suffix, NN)).astype(BF16)


def grad_normed_kernel(cot_ref, w_ref, out_ref):
    block = 1024

    def lap(i, _):
        at = pl.multiple_of(i * block, block)
        part = dot(cot_ref[:, pl.ds(at, block)], w_ref[pl.ds(at, block), :], NN)

        @pl.when(i == 0)
        def _():
            out_ref[...] = part

        @pl.when(i > 0)
        def _():
            out_ref[...] += part

        return 0

    lax.fori_loop(0, cot_ref.shape[1] // block, lap, 0)


def ring_kernel(away, normed_ref, w_ref, *refs):
    group = normed_ref.shape[1]
    _, _, core, z = place_of()
    owner = (z + jnp.where(core == 0, -away, away)) & (NZ - 1)
    rows = pl.ds(pl.multiple_of(owner * group, group), group)
    part = dot(normed_ref[...], w_ref[rows, :], NT)
    for came_ref in refs[:-1]:
        part = part + came_ref[...].astype(F32)
    refs[-1][...] = part.astype(BF16)


def ring_step(away, normed, weight, *came, cost=FREE):
    out = shape(normed.shape, BF16)
    kernel = functools.partial(ring_kernel, away)
    return call(kernel, (out,), normed, weight, *came, cost=cost)[0]


def chip_at(b, a, at):
    y, x, core, _ = at
    row = (y + jnp.where(core == 0, b, a)) & 3
    col = (x + jnp.where(core == 0, a, b)) & 3
    return row * NX + col


def terms_kernel(turned_ref, cot_ref, own_ref, other_ref):
    at = place_of()
    first = at[2] == 0
    cols = own_ref.shape[2]

    def lap(b, _):
        for a in range(4):
            start = pl.multiple_of(chip_at(b, a, at) * (NC * cols), NC * cols)
            res = dot(turned_ref[...], cot_ref[:, pl.ds(start, NC * cols)], NN).astype(BF16)
            lo, hi = res[:, :cols], res[:, cols:]
            own_ref[b * 4 + a] = jnp.where(first, lo, hi)
            other_ref[b * 4 + a] = jnp.where(first, hi, lo)
        return 0

    lax.fori_loop(0, 4, lap, 0)


def terms_of(cotangent, turned):
    chips = NY * NX
    half = shape((chips, turned.shape[0], cotangent.shape[1] // chips // NC), BF16)
    return call(terms_kernel, (half, half), turned, cotangent)


def chip_sum_kernel(own_ref, came_ref, here_ref, up_ref, far_lo_ref, far_hi_ref, down_ref):
    for b in range(4):
        for a in range(4):
            total = own_ref[b * 4 + a].astype(F32) + came_ref[a * 4 + b].astype(F32)
            total = total.astype(BF16)
            if b == 2:
                (far_lo_ref if a < 2 else far_hi_ref)[a % 2] = total
            else:
                (here_ref, up_ref, None, down_ref)[b][a] = total


def relay_kernel(up_ref, down_ref, lo_ref, hi_ref, up_out_ref, down_out_ref):
    for a in range(4):
        if a < 2:
            up_out_ref[a] = (up_ref[a].astype(F32) + lo_ref[a].astype(F32)).astype(BF16)
            down_out_ref[a] = down_ref[a]
        else:
            up_out_ref[a] = up_ref[a]
            down_out_ref[a] = (down_ref[a].astype(F32) + hi_ref[a - 2].astype(F32)).astype(BF16)


def line_sum_kernel(own_ref, *refs):
    came, outs = refs[:2], refs[2:]
    for a in range(4):
        total = own_ref[a].astype(F32)
        for ref in came:
            total = total + ref[a].astype(F32)
        outs[a][...] = total.astype(BF16)


def last_sum_kernel(factor, own_ref, a_ref, b_ref, c_ref, out_ref):
    total = own_ref[...].astype(F32)
    for ref in (a_ref, b_ref, c_ref):
        total = total + ref[...].astype(F32)
    out_ref[...] = total.T * factor


def line_slots(_):
    y, x, core, _ = place_of()
    here = jnp.where(core == 0, x, y)
    return [(here - o) & 3 for o in range(4)]


def gather_slots(other, b):
    y, x, core, _ = place_of()
    core = 1 - core if other else core
    out = []
    for a in range(4):
        row = jnp.where(core == 0, (y + b) & 3, a)
        col = jnp.where(core == 0, a, (x + b) & 3)
        out.append((row * NX + col) * NC + core)
    return out


def place_kernel(rows, counts, slots, lines, *refs):
    out_ref = refs[-1]
    places = [p for line in lines for p in slots(line)]
    n = 0
    for piece, count in zip(refs, counts):
        for i in range(count):
            to = pl.multiple_of(places[n] * rows, rows)
            out_ref[pl.ds(to, rows), :] = piece[i * rows : (i + 1) * rows, :]
            n += 1


def place(rows, total, slots, lines, pieces, into=None, cost=FREE):
    counts = tuple(p.shape[0] // rows for p in pieces)
    kernel = functools.partial(place_kernel, rows, counts, slots, lines)
    out = shape((total, pieces[0].shape[1]), BF16)
    if into is None:
        return call(kernel, (out,), *pieces, cost=cost)[0]
    return call(kernel, (out,), *pieces, into, input_output_aliases={len(pieces): 0})[0]


def scan_begin_kernel(full_ref, came_ref, total_ref, low_ref):
    half = total_ref.shape[0]
    first = place_of()[2] * half
    for h in range(half):
        total = full_ref[first + h] + came_ref[first + h].astype(F32)
        total_ref[h] = total
        low_ref[h] = total.astype(BF16)


def scan_kernel(step, reverse, total_ref, part_ref, came_ref, *outs):
    line = place_of()[0 if step >= 2 else 1]
    behind = (line & 1) if step % 2 == 0 else line >> 1
    counts = (1 - behind if reverse else behind).astype(F32)
    part_out, low_ref = outs[:2]
    for h in range(total_ref.shape[0]):
        came = came_ref[h].astype(F32)
        part = came * counts if step == 0 else part_ref[h] + came * counts
        part_out[h] = part
        if step == 3:
            low_ref[h] = part.astype(BF16)
        else:
            total = total_ref[h] + came
            outs[2][h] = total
            low_ref[h] = total.astype(BF16)


def scan_end_kernel(reverse, part_ref, back_ref, other_ref, out_ref):
    half = part_ref.shape[0]
    core = place_of()[2]
    own = core * half
    counts = (1 - core if reverse else core).astype(F32)
    for h in range(half):
        other = other_ref[own + h].astype(F32) * counts
        out_ref[own + h] = (part_ref[h] + other).astype(BF16)
        other = other_ref[half - own + h].astype(F32) * counts
        out_ref[half - own + h] = (back_ref[h].astype(F32) + other).astype(BF16)


class Scan:

    def __init__(self, reverse):
        self.reverse = reverse

    def begin(self, full, low, *others):
        self.other = send(low, SWAP)
        half = (full.shape[0] // 2, *full.shape[1:])
        self.f32, self.bf16 = shape(half, F32), shape(half, BF16)
        self.total, self.low = call(
            scan_begin_kernel, (self.f32, self.bf16), after(full, *others), self.other
        )
        self.part = self.total

    def step(self, i, first=(), then=(), cost=FREE):
        came = send(after(self.low, *first), SCAN[i])
        outs = (self.f32, self.bf16) + ((self.f32,) if i < 3 else ())
        self.part, self.low, *total = call(
            functools.partial(scan_kernel, i, self.reverse),
            outs,
            after(self.total, *then), self.part, came,
            cost=cost,
        )
        self.total = total[0] if total else None

    def end(self, *others):
        back = send(after(self.low, *others), SWAP)
        return call(
            functools.partial(scan_end_kernel, self.reverse),
            (shape(self.other.shape, BF16),),
            self.part, back, self.other,
        )[0]


def halves_kernel(a_ref, b_ref, lo_ref, hi_ref):
    rows = lo_ref.shape[0]
    lo_ref[...] = a_ref[:rows]
    hi_ref[...] = b_ref[rows:]


def chip_sums(own, came):
    _, width, cols = own.shape
    full, half = shape((4, width, cols), BF16), shape((2, width, cols), BF16)
    return call(chip_sum_kernel, (full, full, half, half, full), own, came)


def line_sums(own, *lines):
    _, width, cols = own.shape
    return call(line_sum_kernel, (shape((width, cols), BF16),) * 4, own, *lines)


def last_sum(lines, factor):
    width, cols = lines[0].shape
    kernel = functools.partial(last_sum_kernel, factor)
    return call(kernel, (shape((cols, width), F32),), *lines)[0]


def body(queries, keys, values, gain, out_weight, cotangent):
    tokens, width = queries.shape
    heads = width // DH
    state = shape((heads, DH, DH), F32)
    state_low = shape((heads, DH, DH), BF16)
    whole_f32 = shape((tokens, width), F32)
    whole_bf16 = shape((tokens, width), BF16)
    gain2 = gain.reshape(1, width)

    rows = out_weight.shape[0]
    came = [send(out_weight, ALONG_A[o]) for o in (1, 2, 3)]
    block = shape(out_weight.shape, BF16)
    full, low, block = call(states_kernel, (state, state_low, block), keys, values, out_weight)
    scan = Scan(False)
    scan.begin(full, low, *came)
    line = place(rows, 4 * rows, line_slots, (0,), [block, after(came[0], scan.low), *came[1:]])
    scan.step(0, cost=LONGEST)
    scan.step(1)
    before, behind = send(line, ALONG_B[1]), send(line, ALONG_B[3])
    (intra,) = call(intra_kernel, (whole_f32,), after(queries, line), keys, values)
    half_line = shape((2 * rows, width), BF16)
    lo, hi = call(halves_kernel, (half_line, half_line), before, behind)
    scan.step(2, (intra,), (lo,))
    scan.step(3, (lo,))
    far_lo, far_hi = send(lo, ALONG_B[1]), send(hi, ALONG_B[3])
    own = [line, before, behind, far_lo, far_hi]
    other = [send(piece, SWAP) for piece in own]
    prefix = scan.end(far_lo, far_hi)
    size = rows * NY * NX * NC
    weight = place(rows, size, functools.partial(gather_slots, False), (0, 3, 1, 2), own)
    weight = place(
        rows, size, functools.partial(gather_slots, True), (0, 3, 1, 2), other, into=weight
    )
    attended, normed, turned = call(
        normed_kernel,
        (whole_f32, whole_bf16, shape((width, tokens), BF16)),
        intra, queries, prefix, gain2,
    )

    long = ring_step(4, normed, weight)
    short = ring_step(-3, normed, weight)
    grad_normed = call(grad_normed_kernel, (whole_f32,), after(cotangent, long, short), weight)[0]
    grad_att, g_full, g_low = call(
        grad_att_kernel, (whole_bf16, state, state_low), grad_normed, attended, gain2, queries
    )
    scan = Scan(True)
    scan.begin(g_full, g_low)
    own, other = terms_of(cotangent, after(turned, scan.total))
    scan.step(0, (), (own,))

    came = send(long, LONG), send(short, SHORT)
    ready = after(normed, scan.total)
    long = ring_step(3, ready, weight, came[0], cost=LONGEST)
    short = ring_step(-2, ready, weight, came[1])
    dk_part, dv_part = call(
        inner_kernel, (whole_f32, whole_f32), queries, keys, values, after(grad_att, long, short)
    )
    scan.step(1, (long, short), (dk_part,))
    here, up, far_lo, far_hi, down = chip_sums(after(own, scan.total), send(other, SWAP))
    far = send(far_lo, ALONG_B[1]), send(far_hi, ALONG_B[3])
    (grad_queries,) = call(
        queries_kernel, (whole_bf16,), keys, values, after(grad_att, here), prefix
    )
    scan.step(2, (), (grad_queries,))

    came = send(long, LONG), send(short, SHORT)
    ready = after(normed, scan.total)
    long = ring_step(2, ready, weight, came[0], cost=LONGEST)
    short = ring_step(-1, ready, weight, came[1])
    up = after(up, long, short)
    up, down = call(relay_kernel, (shape(up.shape, BF16),) * 2, up, down, *far)
    near = send(after(up, long, short), ALONG_B[1]), send(after(down, long, short), ALONG_B[3])
    scan.step(3, (long, short))

    came = send(long, LONG), send(short, SHORT)
    suffix = scan.end()

    came = send(long, LONG), send(short, SHORT)
    ready = after(normed, suffix, came[1])
    long = ring_step(1, ready, weight, came[0])
    grad_keys, grad_values = call(
        finish_kernel, (whole_bf16, whole_bf16), dk_part, dv_part, keys, values, after(suffix, long)
    )
    line = line_sums(after(here, long), *near)
    last = [send(line[o], ALONG_A[o]) for o in (2, 1, 3)]
    layer_out = ring_step(0, normed, weight, send(long, LONG), came[1])
    here = after(line[0], layer_out)
    grad_weight = last_sum([here, *last], (tokens * NY * NX * NC) ** -0.5)
    return (layer_out, grad_queries, grad_keys, grad_values, grad_weight)


def solution(mesh):
    placed = (
        P("seq", "head"),
        P("seq", "head"),
        P("seq", "head"),
        P("head"),
        P("seq", "head"),
        P("seq", None),
    )
    return jax.shard_map(
        body,
        mesh=mesh,
        in_specs=placed,
        out_specs=(P("seq", "head"),) * 5,
        check_vma=False,
    )
```

```python
import functools

import jax
import jax.numpy as jnp
from jax import lax
from jax.experimental import pallas as pl
from jax.experimental.pallas import tpu as pltpu
from jax.sharding import PartitionSpec as P

DH = 128
SPAN = 512
EPS = 1e-06
ROOM = 16 * 2**20
FREE = pl.CostEstimate(flops=0, bytes_accessed=0, transcendentals=0)
LONGEST = pl.CostEstimate(flops=2 * 10**10, bytes_accessed=0, transcendentals=0)
NY, NX, NC, NZ = 4, 4, 2, 8
AXES = ("seq", "head")
F32, BF16 = jnp.float32, jnp.bfloat16
NT = (((1,), (1,)), ((), ()))
NN = (((1,), (0,)), ((), ()))
TN = (((0,), (0,)), ((), ()))


def dot(a, b, dims):
    return lax.dot_general(a, b, dims, preferred_element_type=F32)


def pairs(move):
    out = []
    for y in range(NY):
        for x in range(NX):
            for c in range(NC):
                for z in range(NZ):
                    ty, tx, tc, tz = move(y, x, c, z)
                    here = ((y * NX + x) * NC + c) * NZ + z
                    there = (((ty % NY) * NX + tx % NX) * NC + tc) * NZ + tz % NZ
                    out.append((here, there))
    return out


SWAP = pairs(lambda y, x, c, z: (y, x, 1 - c, z))
SCAN = (
    pairs(lambda y, x, c, z: (y, x ^ 1, c, z)),
    pairs(lambda y, x, c, z: (y, 3 - x, c, z)),
    pairs(lambda y, x, c, z: (y ^ 1, x, c, z)),
    pairs(lambda y, x, c, z: (3 - y, x, c, z)),
)
ALONG_A = {
    o: pairs(lambda y, x, c, z, o=o: (y, x + o, c, z) if c == 0 else (y + o, x, c, z))
    for o in (1, 2, 3)
}
ALONG_B = {
    o: pairs(lambda y, x, c, z, o=o: (y + o, x, c, z) if c == 0 else (y, x + o, c, z))
    for o in (1, 2, 3)
}
LONG = pairs(lambda y, x, c, z: (y, x, c, z - 1 if c == 0 else z + 1))
SHORT = pairs(lambda y, x, c, z: (y, x, c, z + 1 if c == 0 else z - 1))


def send(value, perm):
    return lax.ppermute(value, AXES, perm)


def after(value, *others):
    return lax.optimization_barrier((value, *others))[0]


def whole(n):
    return [pl.BlockSpec(memory_space=pltpu.VMEM)] * n


def call(kernel, outs, *args, cost=FREE, **extra):
    return pl.pallas_call(
        kernel,
        out_shape=tuple(outs),
        in_specs=whole(len(args)),
        out_specs=tuple(whole(len(outs))),
        compiler_params=pltpu.CompilerParams(vmem_limit_bytes=ROOM),
        cost_estimate=cost,
        **extra,
    )(*args)


def place_of():
    s = lax.axis_index("seq")
    return s >> 3, (s >> 1) & 3, s & 1, lax.axis_index("head")


def shape(dims, dtype):
    return jax.ShapeDtypeStruct(dims, dtype)


def head(ref, h, rows=slice(None)):
    return ref[rows, h * DH : (h + 1) * DH]


def states_kernel(k_ref, v_ref, w_ref, full_ref, sent_ref, w_out_ref):
    w_out_ref[...] = w_ref[...]
    for h in range(full_ref.shape[0]):
        state = dot(head(k_ref, h), head(v_ref, h), TN)
        full_ref[h] = state
        sent_ref[h] = state.astype(BF16)


def lower(n):
    return lax.broadcasted_iota(jnp.int32, (n, n), 0) >= lax.broadcasted_iota(jnp.int32, (n, n), 1)


HALF = SPAN // 2


def intra_kernel(q_ref, k_ref, v_ref, out_ref):
    keep = lower(HALF)
    lo, hi = slice(0, HALF), slice(HALF, SPAN)
    for h in range(q_ref.shape[1] // DH):
        k0, k1 = head(k_ref, h, lo), head(k_ref, h, hi)
        v0, v1 = head(v_ref, h, lo), head(v_ref, h, hi)
        q0, q1 = head(q_ref, h, lo), head(q_ref, h, hi)
        s00 = jnp.where(keep, dot(q0, k0, NT), 0.0).astype(BF16)
        s10 = dot(q1, k0, NT).astype(BF16)
        s11 = jnp.where(keep, dot(q1, k1, NT), 0.0).astype(BF16)
        out_ref[lo, h * DH : (h + 1) * DH] = dot(s00, v0, NN)
        out_ref[hi, h * DH : (h + 1) * DH] = dot(s10, v0, NN) + dot(s11, v1, NN)


def normed_kernel(intra_ref, q_ref, prefix_ref, gain_ref, att_ref, normed_ref, turned_ref):
    for h in range(q_ref.shape[1] // DH):
        cols = slice(h * DH, (h + 1) * DH)
        att = intra_ref[:, cols] + dot(q_ref[:, cols], prefix_ref[h], NN)
        att_ref[:, cols] = att
        inv = lax.rsqrt(jnp.mean(att * att, axis=-1, keepdims=True) + EPS)
        normed = (att * inv * gain_ref[:, cols]).astype(BF16)
        normed_ref[:, cols] = normed
        turned_ref[cols, :] = normed.T


def grad_att_kernel(gn_ref, att_ref, gain_ref, q_ref, g_ref, full_ref, sent_ref):
    for h in range(q_ref.shape[1] // DH):
        cols = slice(h * DH, (h + 1) * DH)
        att = att_ref[:, cols]
        inv = lax.rsqrt(jnp.mean(att * att, axis=-1, keepdims=True) + EPS)
        a = gn_ref[:, cols] * gain_ref[:, cols]
        inner = jnp.mean(a * att, axis=-1, keepdims=True)
        g = (inv * (a - att * (inv * inv * inner))).astype(BF16)
        g_ref[:, cols] = g
        state = dot(q_ref[:, cols], g, TN)
        full_ref[h] = state
        sent_ref[h] = state.astype(BF16)


def queries_kernel(k_ref, v_ref, g_ref, prefix_ref, dq_ref):
    keep = lower(HALF)
    lo, hi = slice(0, HALF), slice(HALF, SPAN)
    for h in range(k_ref.shape[1] // DH):
        cols = slice(h * DH, (h + 1) * DH)
        k0, k1 = k_ref[lo, cols], k_ref[hi, cols]
        v0, v1 = v_ref[lo, cols], v_ref[hi, cols]
        g0, g1 = g_ref[lo, cols], g_ref[hi, cols]
        prefix = prefix_ref[h]
        d00 = jnp.where(keep, dot(g0, v0, NT), 0.0).astype(BF16)
        d10 = dot(g1, v0, NT).astype(BF16)
        d11 = jnp.where(keep, dot(g1, v1, NT), 0.0).astype(BF16)
        dq_ref[lo, cols] = (dot(d00, k0, NN) + dot(g0, prefix, NT)).astype(BF16)
        dq_ref[hi, cols] = (dot(d10, k0, NN) + dot(d11, k1, NN) + dot(g1, prefix, NT)).astype(BF16)


def inner_kernel(q_ref, k_ref, v_ref, g_ref, dk_ref, dv_ref):
    upper = lax.broadcasted_iota(jnp.int32, (HALF, HALF), 0) <= lax.broadcasted_iota(
        jnp.int32, (HALF, HALF), 1
    )
    lo, hi = slice(0, HALF), slice(HALF, SPAN)
    for h in range(q_ref.shape[1] // DH):
        cols = slice(h * DH, (h + 1) * DH)
        q0, q1 = q_ref[lo, cols], q_ref[hi, cols]
        k0, k1 = k_ref[lo, cols], k_ref[hi, cols]
        v0, v1 = v_ref[lo, cols], v_ref[hi, cols]
        g0, g1 = g_ref[lo, cols], g_ref[hi, cols]
        e00 = jnp.where(upper, dot(v0, g0, NT), 0.0).astype(BF16)
        e01 = dot(v0, g1, NT).astype(BF16)
        e11 = jnp.where(upper, dot(v1, g1, NT), 0.0).astype(BF16)
        dk_ref[lo, cols] = dot(e00, q0, NN) + dot(e01, q1, NN)
        dk_ref[hi, cols] = dot(e11, q1, NN)
        s00 = jnp.where(upper, dot(k0, q0, NT), 0.0).astype(BF16)
        s01 = dot(k0, q1, NT).astype(BF16)
        s11 = jnp.where(upper, dot(k1, q1, NT), 0.0).astype(BF16)
        dv_ref[lo, cols] = dot(s00, g0, NN) + dot(s01, g1, NN)
        dv_ref[hi, cols] = dot(s11, g1, NN)


def finish_kernel(dk_part_ref, dv_part_ref, k_ref, v_ref, suffix_ref, dk_ref, dv_ref):
    for h in range(k_ref.shape[1] // DH):
        cols = slice(h * DH, (h + 1) * DH)
        suffix = suffix_ref[h]
        dk_ref[:, cols] = (dk_part_ref[:, cols] + dot(v_ref[:, cols], suffix, NT)).astype(BF16)
        dv_ref[:, cols] = (dv_part_ref[:, cols] + dot(k_ref[:, cols], suffix, NN)).astype(BF16)


def grad_normed_kernel(cot_ref, w_ref, out_ref):
    block = 1024

    def lap(i, _):
        at = pl.multiple_of(i * block, block)
        part = dot(cot_ref[:, pl.ds(at, block)], w_ref[pl.ds(at, block), :], NN)

        @pl.when(i == 0)
        def _():
            out_ref[...] = part

        @pl.when(i > 0)
        def _():
            out_ref[...] += part

        return 0

    lax.fori_loop(0, cot_ref.shape[1] // block, lap, 0)


def ring_kernel(away, normed_ref, w_ref, *refs):
    group = normed_ref.shape[1]
    _, _, core, z = place_of()
    owner = (z + jnp.where(core == 0, -away, away)) & (NZ - 1)
    rows = pl.ds(pl.multiple_of(owner * group, group), group)
    part = dot(normed_ref[...], w_ref[rows, :], NT)
    for came_ref in refs[:-1]:
        part = part + came_ref[...].astype(F32)
    refs[-1][...] = part.astype(BF16)


def ring_step(away, normed, weight, *came, cost=FREE):
    out = shape(normed.shape, BF16)
    kernel = functools.partial(ring_kernel, away)
    return call(kernel, (out,), normed, weight, *came, cost=cost)[0]


def chip_at(b, a, at):
    y, x, core, _ = at
    row = (y + jnp.where(core == 0, b, a)) & 3
    col = (x + jnp.where(core == 0, a, b)) & 3
    return row * NX + col


def terms_kernel(turned_ref, cot_ref, own_ref, other_ref):
    at = place_of()
    first = at[2] == 0
    cols = own_ref.shape[2]

    def lap(b, _):
        for a in range(4):
            start = pl.multiple_of(chip_at(b, a, at) * (NC * cols), NC * cols)
            res = dot(turned_ref[...], cot_ref[:, pl.ds(start, NC * cols)], NN).astype(BF16)
            lo, hi = res[:, :cols], res[:, cols:]
            own_ref[b * 4 + a] = jnp.where(first, lo, hi)
            other_ref[b * 4 + a] = jnp.where(first, hi, lo)
        return 0

    lax.fori_loop(0, 4, lap, 0)


def terms_of(cotangent, turned):
    chips = NY * NX
    half = shape((chips, turned.shape[0], cotangent.shape[1] // chips // NC), BF16)
    return call(terms_kernel, (half, half), turned, cotangent)


def chip_sum_kernel(own_ref, came_ref, here_ref, up_ref, far_lo_ref, far_hi_ref, down_ref):
    for b in range(4):
        for a in range(4):
            total = own_ref[b * 4 + a].astype(F32) + came_ref[a * 4 + b].astype(F32)
            total = total.astype(BF16)
            if b == 2:
                (far_lo_ref if a < 2 else far_hi_ref)[a % 2] = total
            else:
                (here_ref, up_ref, None, down_ref)[b][a] = total


def relay_kernel(up_ref, down_ref, lo_ref, hi_ref, up_out_ref, down_out_ref):
    for a in range(4):
        if a < 2:
            up_out_ref[a] = (up_ref[a].astype(F32) + lo_ref[a].astype(F32)).astype(BF16)
            down_out_ref[a] = down_ref[a]
        else:
            up_out_ref[a] = up_ref[a]
            down_out_ref[a] = (down_ref[a].astype(F32) + hi_ref[a - 2].astype(F32)).astype(BF16)


def line_sum_kernel(own_ref, *refs):
    came, outs = refs[:2], refs[2:]
    for a in range(4):
        total = own_ref[a].astype(F32)
        for ref in came:
            total = total + ref[a].astype(F32)
        outs[a][...] = total.astype(BF16)


def last_sum_kernel(factor, own_ref, a_ref, b_ref, c_ref, out_ref):
    total = own_ref[...].astype(F32)
    for ref in (a_ref, b_ref, c_ref):
        total = total + ref[...].astype(F32)
    out_ref[...] = total.T * factor


def line_slots(_):
    y, x, core, _ = place_of()
    here = jnp.where(core == 0, x, y)
    return [(here - o) & 3 for o in range(4)]


def gather_slots(other, b):
    y, x, core, _ = place_of()
    core = 1 - core if other else core
    out = []
    for a in range(4):
        row = jnp.where(core == 0, (y + b) & 3, a)
        col = jnp.where(core == 0, a, (x + b) & 3)
        out.append((row * NX + col) * NC + core)
    return out


def place_kernel(rows, counts, slots, lines, *refs):
    out_ref = refs[-1]
    places = [p for line in lines for p in slots(line)]
    n = 0
    for piece, count in zip(refs, counts):
        for i in range(count):
            to = pl.multiple_of(places[n] * rows, rows)
            out_ref[pl.ds(to, rows), :] = piece[i * rows : (i + 1) * rows, :]
            n += 1


def place(rows, total, slots, lines, pieces, into=None, cost=FREE):
    counts = tuple(p.shape[0] // rows for p in pieces)
    kernel = functools.partial(place_kernel, rows, counts, slots, lines)
    out = shape((total, pieces[0].shape[1]), BF16)
    if into is None:
        return call(kernel, (out,), *pieces, cost=cost)[0]
    return call(kernel, (out,), *pieces, into, input_output_aliases={len(pieces): 0})[0]


def scan_begin_kernel(full_ref, came_ref, total_ref, low_ref):
    half = total_ref.shape[0]
    first = place_of()[2] * half
    for h in range(half):
        total = full_ref[first + h] + came_ref[first + h].astype(F32)
        total_ref[h] = total
        low_ref[h] = total.astype(BF16)


def scan_kernel(step, reverse, total_ref, part_ref, came_ref, *outs):
    line = place_of()[0 if step >= 2 else 1]
    behind = (line & 1) if step % 2 == 0 else line >> 1
    counts = (1 - behind if reverse else behind).astype(F32)
    part_out, low_ref = outs[:2]
    for h in range(total_ref.shape[0]):
        came = came_ref[h].astype(F32)
        part = came * counts if step == 0 else part_ref[h] + came * counts
        part_out[h] = part
        if step == 3:
            low_ref[h] = part.astype(BF16)
        else:
            total = total_ref[h] + came
            outs[2][h] = total
            low_ref[h] = total.astype(BF16)


def scan_end_kernel(reverse, part_ref, back_ref, other_ref, out_ref):
    half = part_ref.shape[0]
    core = place_of()[2]
    own = core * half
    counts = (1 - core if reverse else core).astype(F32)
    for h in range(half):
        other = other_ref[own + h].astype(F32) * counts
        out_ref[own + h] = (part_ref[h] + other).astype(BF16)
        other = other_ref[half - own + h].astype(F32) * counts
        out_ref[half - own + h] = (back_ref[h].astype(F32) + other).astype(BF16)


class Scan:

    def __init__(self, reverse):
        self.reverse = reverse

    def begin(self, full, low, *others):
        self.other = send(low, SWAP)
        half = (full.shape[0] // 2, *full.shape[1:])
        self.f32, self.bf16 = shape(half, F32), shape(half, BF16)
        self.total, self.low = call(
            scan_begin_kernel, (self.f32, self.bf16), after(full, *others), self.other
        )
        self.part = self.total

    def step(self, i, first=(), then=(), cost=FREE):
        came = send(after(self.low, *first), SCAN[i])
        outs = (self.f32, self.bf16) + ((self.f32,) if i < 3 else ())
        self.part, self.low, *total = call(
            functools.partial(scan_kernel, i, self.reverse),
            outs,
            after(self.total, *then), self.part, came,
            cost=cost,
        )
        self.total = total[0] if total else None

    def end(self, *others):
        back = send(after(self.low, *others), SWAP)
        return call(
            functools.partial(scan_end_kernel, self.reverse),
            (shape(self.other.shape, BF16),),
            self.part, back, self.other,
        )[0]


def halves_kernel(a_ref, b_ref, lo_ref, hi_ref):
    rows = lo_ref.shape[0]
    lo_ref[...] = a_ref[:rows]
    hi_ref[...] = b_ref[rows:]


def chip_sums(own, came):
    _, width, cols = own.shape
    full, half = shape((4, width, cols), BF16), shape((2, width, cols), BF16)
    return call(chip_sum_kernel, (full, full, half, half, full), own, came)


def line_sums(own, *lines):
    _, width, cols = own.shape
    return call(line_sum_kernel, (shape((width, cols), BF16),) * 4, own, *lines)


def last_sum(lines, factor):
    width, cols = lines[0].shape
    kernel = functools.partial(last_sum_kernel, factor)
    return call(kernel, (shape((cols, width), F32),), *lines)[0]


def body(queries, keys, values, gain, out_weight, cotangent):
    tokens, width = queries.shape
    heads = width // DH
    state = shape((heads, DH, DH), F32)
    state_low = shape((heads, DH, DH), BF16)
    whole_f32 = shape((tokens, width), F32)
    whole_bf16 = shape((tokens, width), BF16)
    gain2 = gain.reshape(1, width)

    rows = out_weight.shape[0]
    came = [send(out_weight, ALONG_A[o]) for o in (1, 2, 3)]
    block = shape(out_weight.shape, BF16)
    full, low, block = call(states_kernel, (state, state_low, block), keys, values, out_weight)
    scan = Scan(False)
    scan.begin(full, low, *came)
    line = place(rows, 4 * rows, line_slots, (0,), [block, after(came[0], scan.low), *came[1:]])
    scan.step(0, cost=LONGEST)
    scan.step(1)
    before, behind = send(line, ALONG_B[1]), send(line, ALONG_B[3])
    (intra,) = call(intra_kernel, (whole_f32,), after(queries, line), keys, values)
    half_line = shape((2 * rows, width), BF16)
    lo, hi = call(halves_kernel, (half_line, half_line), before, behind)
    scan.step(2, (intra,), (lo,))
    scan.step(3, (lo,))
    far_lo, far_hi = send(lo, ALONG_B[1]), send(hi, ALONG_B[3])
    own = [line, before, behind, far_lo, far_hi]
    other = [send(piece, SWAP) for piece in own]
    prefix = scan.end(far_lo, far_hi)
    size = rows * NY * NX * NC
    weight = place(rows, size, functools.partial(gather_slots, False), (0, 3, 1, 2), own)
    weight = place(
        rows, size, functools.partial(gather_slots, True), (0, 3, 1, 2), other, into=weight
    )
    attended, normed, turned = call(
        normed_kernel,
        (whole_f32, whole_bf16, shape((width, tokens), BF16)),
        intra, queries, prefix, gain2,
    )

    long = ring_step(4, normed, weight)
    short = ring_step(-3, normed, weight)
    grad_normed = call(grad_normed_kernel, (whole_f32,), after(cotangent, long, short), weight)[0]
    grad_att, g_full, g_low = call(
        grad_att_kernel, (whole_bf16, state, state_low), grad_normed, attended, gain2, queries
    )
    scan = Scan(True)
    scan.begin(g_full, g_low)
    own, other = terms_of(cotangent, after(turned, scan.total))
    scan.step(0, (), (own,))

    came = send(long, LONG), send(short, SHORT)
    ready = after(normed, scan.total)
    long = ring_step(3, ready, weight, came[0], cost=LONGEST)
    short = ring_step(-2, ready, weight, came[1])
    here, up, far_lo, far_hi, down = chip_sums(own, send(other, SWAP))
    far = send(far_lo, ALONG_B[1]), send(far_hi, ALONG_B[3])
    dk_part, dv_part = call(
        inner_kernel, (whole_f32, whole_f32), queries, keys, values, after(grad_att, here)
    )
    scan.step(1, (long, short), (dk_part,))
    (grad_queries,) = call(
        queries_kernel, (whole_bf16,), keys, values, after(grad_att, scan.total), prefix
    )
    scan.step(2, (), (grad_queries,))
    up, down = call(relay_kernel, (shape(up.shape, BF16),) * 2, up, down, *far)

    came = send(long, LONG), send(short, SHORT)
    ready = after(normed, scan.total, up)
    long = ring_step(2, ready, weight, came[0], cost=LONGEST)
    short = ring_step(-1, ready, weight, came[1])
    near = send(after(up, long, short), ALONG_B[1]), send(after(down, long, short), ALONG_B[3])
    scan.step(3, (long, short))

    came = send(long, LONG), send(short, SHORT)
    suffix = scan.end()

    came = send(long, LONG), send(short, SHORT)
    ready = after(normed, suffix, came[1])
    long = ring_step(1, ready, weight, came[0])
    grad_keys, grad_values = call(
        finish_kernel, (whole_bf16, whole_bf16), dk_part, dv_part, keys, values, after(suffix, long)
    )
    line = line_sums(after(here, long), *near)
    last = [send(line[o], ALONG_A[o]) for o in (2, 1, 3)]
    layer_out = ring_step(0, normed, weight, send(long, LONG), came[1])
    here = after(line[0], layer_out)
    grad_weight = last_sum([here, *last], (tokens * NY * NX * NC) ** -0.5)
    return (layer_out, grad_queries, grad_keys, grad_values, grad_weight)


def solution(mesh):
    placed = (
        P("seq", "head"),
        P("seq", "head"),
        P("seq", "head"),
        P("head"),
        P("seq", "head"),
        P("seq", None),
    )
    return jax.shard_map(
        body,
        mesh=mesh,
        in_specs=placed,
        out_specs=(P("seq", "head"),) * 5,
        check_vma=False,
    )
```
